128 devices in a mesh: row: 8 (over x, core), col: 16 (over z, y).
Axes of the slice: x: 4, y: 4, z: 4, core: 2. Of those that a mesh axis runs over, the one named last changes fastest.
Arguments:
- traces: bfloat16 [16384, 2, 2048], P(('row', 'col')), may hold values from -6 to 6
- band_taper: float32 [512], replicated, may hold values from 0.25 to 1.75
- pair_first: int32 [131072], P(('row', 'col')), may hold values from 0 to 2047
- pair_second: int32 [131072], P(('row', 'col')), may hold values from 0 to 1023
- pair_owner: int32 [131072, 1], P(('row', 'col')), may hold values from 0 to 15; in each aligned block of 1024 rows (0 to 1023, 1024 to 2047, ...) at most 96 rows name the same one
Outputs:
- stacks: bfloat16 [196608, 2048], P(('row', 'col'))
The draws below stay inside these ranges and needn't reach their ends.
Inputs may be any that keep to these rules, and one draw needn't show every extreme that they name: `pair_owner`: one device's 1024 pairs name each owner at most 96 times.
All inputs are finite; a program needn't handle non-finite values.
Results may differ from the reference program's by a relative error of at most 0.0082.
Values may be sent and summed in bfloat16 or wider, within the bound.
No kernel may reach another device: no remote copies, remote signals or barrier semaphores. Data moves between devices by JAX's collectives and lax.ppermute only.
A program may use at most 128 MiB of HBM per device.

```python
import math
import jax
import jax.numpy as jnp
import numpy as np
from jax import lax

L = 2048
BINS = 512
LOW_BIN = 8
WHITEN_BINS = 64
SEGMENTS = 2
STA_DEV = 128
PAIRS = 1024
CAP = 96
STATIONS = 16384
N_ROW = 8
N_COL = 16
DEVICES = 128


def with_ends(entries, stream_key, smallest, top_value):
    longest = entries.shape.index(max(entries.shape))
    spots = []
    for shift in (0, 1):
        where = [jax.random.randint(jax.random.fold_in(stream_key, axis), (), 0, length) for axis, length in enumerate(entries.shape)]
        where[longest] = (where[longest] + shift) % entries.shape[longest]
        spots.append(tuple(where))
    return entries.at[spots[0]].set(smallest).at[spots[1]].set(top_value)


def block_levels(own_key, extent, cuts, least, largest):
    factor_of, own = 1.0, jax.random.fold_in(own_key, 6)
    for position, parts in cuts:
        steps = jnp.exp(jax.random.uniform(jax.random.fold_in(own, position), (parts,), jnp.float32, least / len(cuts), largest / len(cuts)))
        factor_of = factor_of * jnp.repeat(steps, extent[position] // parts).reshape([-1 if axis == position else 1 for axis in range(len(extent))])
    return factor_of


def deal_out(own_key, own, number, rows, count, top, most, lean):
    order = jax.random.permutation(own_key, count)
    heavy_load, usual = load_shares(count, rows * top, most, lean, True), load_shares(count, rows * top, most, lean, False)
    places = jnp.arange(count)

    def named(tallies, rotation):
        used = int((tallies > 0).sum())
        fixed = max(1, used // 4)
        passed = fixed + (places - fixed + rotation * (used - fixed)) % max(1, count - fixed)
        return jnp.zeros((count,), jnp.int32).at[order[jnp.where(places < fixed, places, passed)]].set(jnp.asarray(tallies, jnp.int32))

    tallies = jnp.where(number % 4 == 0, named(heavy_load, number // 4), named(usual, number - number // 4 - 1))
    mixed = jax.random.permutation(jax.random.fold_in(own, 3), count)
    giver, taker = mixed[0:count // 2 * 2:2], mixed[1:count // 2 * 2:2]
    slack = jnp.minimum(tallies[giver] - 1, most - tallies[taker]) // 2
    slack = jnp.where((giver == order[0]) | (taker == order[0]) | (tallies[taker] == 0), 0, jnp.maximum(slack, 0))
    passed = jax.random.randint(jax.random.fold_in(own, 4), (count // 2,), 0, 1 << 20) % (slack + 1)
    tallies = tallies.at[giver].add(-passed).at[taker].add(passed)
    members = jnp.searchsorted(jnp.cumsum(tallies), jnp.arange(rows * top), side="right").astype(jnp.int32)
    listing = members.reshape(top, rows).T
    listing = listing[jax.random.permutation(jax.random.fold_in(own, 1), rows)]
    rotation = jax.random.randint(jax.random.fold_in(own, 2), (rows, 1), 0, top)
    return jnp.take_along_axis(listing, (jnp.arange(top)[None, :] + rotation) % top, axis=1)


def load_shares(count, total, reach, slope, full):
    portions = [(1 << 20) // math.isqrt(grade ** slope) + 1 for grade in range(1, count + 1)]
    largest = reach if full else min(reach, max(-(-total // count), total * portions[0] // sum(portions)))
    least = 1 if total - largest >= count - 1 else 0
    counts, rest = [largest] + [least] * (count - 1), total - largest - least * (count - 1)
    while rest > 0:
        candidates = [i for i in range(1, count) if counts[i] < largest] or [i for i in range(1, count) if counts[i] < reach]
        mass, remaining = sum([portions[i] for i in candidates]), rest
        for i in candidates:
            addition = min(reach - counts[i], max(1, remaining * portions[i] // mass), rest)
            counts[i] = counts[i] + addition
            rest = rest - addition
    return np.array(counts)


def bell_draw(stream_key, extent, deviation, most, pieces=(), kind=jnp.bfloat16):
    gain = block_levels(stream_key, extent, pieces, -0.22, 0.18) if pieces else 1.0
    values = jax.random.normal(stream_key, extent, jnp.float32) * deviation * gain
    return jnp.minimum(jnp.maximum(values, -most), most).astype(kind)


def setup_inputs(seed: int = 0) -> dict:
    splits = jax.random.split(jax.random.key(seed), 6)
    traces = bell_draw(splits[0], (STATIONS, SEGMENTS, L), 1.0, 6.0, ((0, 128),))
    band_taper = jnp.clip(1.0 + 0.15 * jax.random.normal(splits[1], (BINS,), jnp.float32), 0.25, 1.75)
    pair_first = with_ends(jax.random.randint(splits[2], (DEVICES * PAIRS,), 0, N_COL * STA_DEV), jax.random.fold_in(splits[2], 1), 0, (N_COL * STA_DEV) - 1).astype(jnp.int32)
    pair_second = with_ends(jax.random.randint(splits[3], (DEVICES * PAIRS,), 0, N_ROW * STA_DEV), jax.random.fold_in(splits[3], 1), 0, (N_ROW * STA_DEV) - 1).astype(jnp.int32)
    pair_owner_keys = jax.random.split(jax.random.fold_in(splits[4], 1), (DEVICES * PAIRS) // PAIRS)
    pair_owner_turns = jax.random.permutation(jax.random.fold_in(splits[4], 3), (DEVICES * PAIRS) // PAIRS)
    pair_owner = jax.vmap(lambda own, number: deal_out(jax.random.fold_in(splits[4], 2), own, number, PAIRS, N_COL, 1, CAP, 1))(pair_owner_keys, pair_owner_turns).reshape((DEVICES * PAIRS, 1))
    return dict(traces=traces, band_taper=band_taper, pair_first=pair_first, pair_second=pair_second, pair_owner=pair_owner)


def forward_table():
    sample_index = jnp.arange(L, dtype=jnp.int32)[:, None]
    freq_index = LOW_BIN + jnp.arange(BINS, dtype=jnp.int32)[None, :]
    phase = (sample_index * freq_index % L).astype(jnp.float32) * (2.0 * math.pi / L)
    factor = 1.0 / math.sqrt(L)
    return jnp.concatenate([jnp.cos(phase) * factor, -jnp.sin(phase) * factor], 1).astype(jnp.bfloat16)

def inverse_table():
    freq_index = LOW_BIN + jnp.arange(BINS, dtype=jnp.int32)[:, None]
    sample_index = jnp.arange(L, dtype=jnp.int32)[None, :]
    phase = (sample_index * freq_index % L).astype(jnp.float32) * (2.0 * math.pi / L)
    factor = 1.0 / math.sqrt(BINS)
    return jnp.concatenate([jnp.cos(phase) * factor, -jnp.sin(phase) * factor], 0).astype(jnp.bfloat16)

def whiten(traces):
    station_count = traces.shape[0]
    records = traces.reshape(-1, L)
    spectrum = jnp.dot(records, forward_table(), preferred_element_type=jnp.float32)
    real_part = spectrum[:, :BINS]
    imag_part = spectrum[:, BINS:]
    power = (real_part * real_part + imag_part * imag_part).reshape(-1, BINS // WHITEN_BINS, WHITEN_BINS)
    scaling = lax.rsqrt(lax.optimization_barrier(jnp.mean(power, axis=-1, keepdims=True)) + 1e-06)
    scaling = jnp.broadcast_to(scaling, power.shape).reshape(-1, BINS)
    whitened = jnp.concatenate([real_part * scaling, imag_part * scaling], 1).astype(jnp.bfloat16)
    return whitened.reshape(station_count, SEGMENTS, 2 * BINS)

def correlate(first_rows, second_rows, band_taper):
    first_rows = first_rows.astype(jnp.float32)
    second_rows = second_rows.astype(jnp.float32)
    first_real = first_rows[:, :, :BINS]
    first_imag = first_rows[:, :, BINS:]
    second_real = second_rows[:, :, :BINS]
    second_imag = second_rows[:, :, BINS:]
    cross_real = lax.optimization_barrier(jnp.sum(first_real * second_real + first_imag * second_imag, axis=1))
    cross_imag = lax.optimization_barrier(jnp.sum(first_real * second_imag - first_imag * second_real, axis=1))
    return jnp.concatenate([cross_real * band_taper, cross_imag * band_taper], 1).astype(jnp.bfloat16)

def owner_ranks(owners, count):
    onehot = (owners[:, None] == jnp.arange(count, dtype=jnp.int32)[None, :]).astype(jnp.int32)
    running = jnp.cumsum(onehot, axis=0)
    return lax.optimization_barrier(jnp.sum(running * onehot, axis=1)).astype(jnp.int32) - 1

def reference(traces, band_taper, pair_first, pair_second, pair_owner):
    whitened = whiten(traces)
    inverse = inverse_table()
    slots = N_COL * CAP

    def one_device(device):
        row_index = device // N_COL
        col_index = device % N_COL
        first_local = lax.dynamic_slice_in_dim(pair_first, device * PAIRS, PAIRS)
        second_local = lax.dynamic_slice_in_dim(pair_second, device * PAIRS, PAIRS)
        owners = lax.dynamic_slice_in_dim(pair_owner[:, 0], device * PAIRS, PAIRS)
        first_station = row_index * N_COL * STA_DEV + first_local
        second_station = (second_local // STA_DEV * N_COL + col_index) * STA_DEV + second_local % STA_DEV
        cross = correlate(whitened[first_station], whitened[second_station], band_taper)
        lags = jnp.dot(cross, inverse, preferred_element_type=jnp.float32).astype(jnp.bfloat16)
        ranks = owner_ranks(owners, N_COL)
        target = (row_index * N_COL + owners) * slots + col_index * CAP + ranks
        return (lags, target.astype(jnp.int32))
    lags, target = lax.map(one_device, jnp.arange(DEVICES, dtype=jnp.int32))
    stacks = jnp.zeros((DEVICES * slots, L), jnp.bfloat16)
    return stacks.at[target.reshape(-1)].set(lags.reshape(-1, L))
```

```python
import functools
import math

import jax
import jax.numpy as jnp
import ml_dtypes
import numpy as np
from jax import lax
from jax.experimental import pallas as pl
from jax.experimental.pallas import tpu as pltpu
from jax.sharding import PartitionSpec as P

L = 2048
BINS = 512
LOW_BIN = 8
STA = 128
CAP = 96
SIDE = 4
OWNERS = 16
PAIRS = 1024
HALF_ROWS = STA * 16 // 2

EVEN = np.arange(0, BINS, 2)
ODD = np.arange(1, BINS, 2)


def forward_tables():
    t = np.arange(L)[:, None]
    k = LOW_BIN + np.arange(BINS)[None, :]
    phase = (t * k % L) * (2.0 * math.pi / L)
    re = np.cos(phase) / math.sqrt(L)
    im = -np.sin(phase) / math.sqrt(L)
    steps = []
    for g in range(2):
        e, o = EVEN[g * 128 : (g + 1) * 128], ODD[g * 128 : (g + 1) * 128]
        steps.append(np.concatenate([re[:, e], re[:, o], im[:, e], im[:, o]], 1))
    return np.stack(steps).astype(np.float32).astype(ml_dtypes.bfloat16)


def inverse_tables():
    t = np.arange(L // 2)[None, :]
    k = LOW_BIN + np.arange(BINS)[:, None]
    phase = (t * k % L) * (2.0 * math.pi / L)
    re = np.cos(phase) / math.sqrt(BINS)
    im = -np.sin(phase) / math.sqrt(BINS)
    even = np.concatenate([re[EVEN], im[EVEN]], 0)
    odd = np.concatenate([re[ODD], im[ODD]], 0)
    return np.stack([even, odd]).astype(np.float32).astype(ml_dtypes.bfloat16)


def whiten_kernel(x_ref, table_ref, first_ref, second_ref, whole_ref, rows_ref):
    g = pl.program_id(0)
    spectrum = jnp.dot(x_ref[...], table_ref[0], preferred_element_type=jnp.float32)
    parts = [spectrum[:, i * 128 : (i + 1) * 128] for i in range(4)]
    power = sum(p * p for p in parts)
    lane_r = lax.broadcasted_iota(jnp.int32, (128, 128), 0)
    lane_c = lax.broadcasted_iota(jnp.int32, (128, 128), 1)
    group = jnp.where((lane_r >> 5) == (lane_c >> 5), 1.0 / 64.0, 0.0).astype(jnp.float32)
    mean = jnp.dot(
        power, group, preferred_element_type=jnp.float32, precision=lax.Precision.HIGHEST
    )
    scaling = lax.rsqrt(mean + 1e-06)
    for i, p in enumerate(parts):
        rows_ref[pl.ds(2 * i + g, 2 * STA, stride=8), :] = p * scaling

    @pl.when(g == 1)
    def _():
        whole = rows_ref[...].astype(jnp.bfloat16)
        first_ref[...] = whole[:HALF_ROWS]
        second_ref[...] = whole[HALF_ROWS:]
        whole_ref[...] = whole


def whiten(records):
    half = jax.ShapeDtypeStruct((HALF_ROWS, 128), jnp.bfloat16)
    whole = jax.ShapeDtypeStruct((2 * HALF_ROWS, 128), jnp.bfloat16)
    return pl.pallas_call(
        whiten_kernel,
        grid=(2,),
        out_shape=(half, half, whole),
        in_specs=[
            pl.BlockSpec((2 * STA, L), lambda g: (0, 0)),
            pl.BlockSpec((1, L, 512), lambda g: (g, 0, 0)),
        ],
        out_specs=(
            pl.BlockSpec((HALF_ROWS, 128), lambda g: (0, 0)),
            pl.BlockSpec((HALF_ROWS, 128), lambda g: (0, 0)),
            pl.BlockSpec((2 * HALF_ROWS, 128), lambda g: (0, 0)),
        ),
        scratch_shapes=[pltpu.VMEM((2 * HALF_ROWS, 128), jnp.float32)],
        compiler_params=pltpu.CompilerParams(vmem_limit_bytes=32 * 1024 * 1024),
        cost_estimate=pl.CostEstimate(
            flops=2 * 256 * L * 1024, bytes_accessed=6 * 2**20, transcendentals=0
        ),
        name="whiten",
    )(records, jnp.asarray(forward_tables()))


def shift(value, axis, step):
    pairs = []
    for z in range(SIDE):
        for y in range(SIDE):
            to = (z * SIDE + (y + step) % SIDE) if axis == "y" else ((z + step) % SIDE) * SIDE + y
            pairs.append((z * SIDE + y, to))
    return lax.ppermute(value, "col", pairs)


def ring(value, axis):
    half = value.shape[0] // 2
    before = shift(value, axis, 1)
    after = shift(value, axis, -1)
    low = shift(before[:half], axis, 1)
    high = shift(after[half:], axis, -1)
    return value, before, after, low, high


def cross_kernel(first_ref, second_ref, slot_ref, taper_ref, *refs):
    pieces, b_hbm, out_ref, a_ref, b_ref, cross_ref, sems = (
        refs[:10],
        refs[10],
        refs[11],
        refs[12],
        refs[13],
        refs[14],
        refs[15],
    )
    copies = [pltpu.make_async_copy(b_hbm, b_ref, sems.at[10])]
    at = 0
    for i, piece in enumerate(pieces):
        rows = piece.shape[0]
        copies.append(pltpu.make_async_copy(piece, a_ref.at[pl.ds(at, rows), :], sems.at[i]))
        at += rows
    for copy in copies:
        copy.start()
    cross_ref[...] = jnp.zeros_like(cross_ref)
    for copy in copies:
        copy.wait()
    taper = taper_ref[...]
    low = lax.broadcasted_iota(jnp.int32, (8, 128), 0) < 4
    signed = jnp.where(low, taper, -taper)
    unroll = 8

    def step(i, carry):
        for u in range(unroll):
            p = i * unroll + u
            a = a_ref[pl.ds(pl.multiple_of(first_ref[p] * 16, 16), 16), :].astype(jnp.float32)
            b = b_ref[pl.ds(pl.multiple_of(second_ref[p] * 16, 16), 16), :].astype(jnp.float32)
            a0, a1, b0, b1 = a[:8], a[8:], b[:8], b[8:]
            same = a0 * b0 + a1 * b1
            swapped = a0 * pltpu.roll(b0, 4, 0) + a1 * pltpu.roll(b1, 4, 0)
            keep = jnp.where(low, same, swapped)
            move = jnp.where(low, swapped, same)
            value = keep * signed + pltpu.roll(move, 4, 0) * taper
            cross_ref[pl.ds(slot_ref[p], 8, stride=CAP), :] = value
        return carry

    lax.fori_loop(0, PAIRS // unroll, step, 0)
    out_ref[...] = cross_ref[...].astype(jnp.bfloat16)


def cross_rows(first, second, slot, taper, pieces, b):
    smem = pl.BlockSpec(memory_space=pltpu.SMEM)
    rows = OWNERS * CAP * 8
    return pl.pallas_call(
        cross_kernel,
        out_shape=jax.ShapeDtypeStruct((rows, 128), jnp.bfloat16),
        in_specs=[smem, smem, smem, pl.BlockSpec(memory_space=pltpu.VMEM)]
        + [pl.BlockSpec(memory_space=pl.ANY)] * 11,
        out_specs=pl.BlockSpec(memory_space=pltpu.VMEM),
        scratch_shapes=[
            pltpu.VMEM((2048 * 16, 128), jnp.bfloat16),
            pltpu.VMEM((1024 * 16, 128), jnp.bfloat16),
            pltpu.VMEM((rows, 128), jnp.float32),
            pltpu.SemaphoreType.DMA((11,)),
        ],
        compiler_params=pltpu.CompilerParams(vmem_limit_bytes=40 * 1024 * 1024),
        cost_estimate=pl.CostEstimate(
            flops=16 * 1024 * 1024, bytes_accessed=15 * 2**20, transcendentals=0
        ),
        name="cross",
    )(first, second, slot, taper, *pieces, b)


def inverse_kernel(cross_ref, table_ref, out_ref):
    sources = cross_ref.shape[0]

    def rows(columns):
        blocks = []
        for s in range(sources):
            parts = [cross_ref[s, j * CAP : (j + 1) * CAP, :] for j in columns]
            blocks.append(jnp.concatenate(parts, 1))
        return jnp.concatenate(blocks, 0)

    even, odd = rows((0, 1, 4, 5)), rows((2, 3, 6, 7))
    width = 256
    for n in range(0, L // 2, width):
        e = jnp.dot(even, table_ref[0, :, n : n + width], preferred_element_type=jnp.float32)
        o = jnp.dot(odd, table_ref[1, :, n : n + width], preferred_element_type=jnp.float32)
        out_ref[:, n : n + width] = (e + o).astype(jnp.bfloat16)
        out_ref[:, L // 2 + n : L // 2 + n + width] = (e - o).astype(jnp.bfloat16)


def inverse(arrived):
    block = 4
    return pl.pallas_call(
        inverse_kernel,
        grid=(OWNERS // block,),
        out_shape=jax.ShapeDtypeStruct((OWNERS * CAP, L), jnp.bfloat16),
        in_specs=[
            pl.BlockSpec((block, 8 * CAP, 128), lambda i: (i, 0, 0)),
            pl.BlockSpec((2, BINS, L // 2), lambda i: (0, 0, 0)),
        ],
        out_specs=pl.BlockSpec((block * CAP, L), lambda i: (i, 0)),
        compiler_params=pltpu.CompilerParams(vmem_limit_bytes=32 * 1024 * 1024),
        cost_estimate=pl.CostEstimate(
            flops=2 * 1536 * 1024 * 1024, bytes_accessed=11 * 2**20, transcendentals=0
        ),
        name="inverse",
    )(arrived, jnp.asarray(inverse_tables()))


def body(traces, band_taper, pair_first, pair_second, pair_owner):
    first_half, second_half, whole = whiten(traces.reshape(2 * STA, L))
    b = lax.all_gather(whole, "row", axis=0, tiled=True)
    over_y = jnp.concatenate(ring(first_half, "y"), 0)
    over_z = jnp.concatenate(ring(second_half, "z"), 0)
    pieces = ring(over_y, "z") + ring(over_z, "y")

    me = lax.axis_index("col")
    home = pair_first >> 7
    local = pair_first & 127
    away_z = ((home >> 2) - (me >> 2)) & 3
    away_y = ((home & 3) - (me & 3)) & 3
    place_z = jnp.where(away_z == 0, 0, jnp.where(away_z == 3, 1, away_z + 1))
    place_y = jnp.where(away_y == 0, 0, jnp.where(away_y == 3, 1, away_y + 1))
    block = jnp.where(local < 64, place_z * SIDE + place_y, 16 + place_y * SIDE + place_z)
    first = block * 64 + (local & 63)

    owners = pair_owner[:, 0]
    index = jnp.arange(PAIRS, dtype=jnp.int32)
    earlier = (owners[:, None] == owners[None, :]) & (index[None, :] < index[:, None])
    rank = jnp.sum(earlier.astype(jnp.int32), axis=1)
    slot = owners * (8 * CAP) + rank

    by_parity = band_taper.reshape(BINS // 2, 2).T.reshape(4, 128)
    taper = jnp.concatenate([by_parity, by_parity], 0)

    cross = cross_rows(first, pair_second, slot, taper, pieces, b)
    outgoing = cross.reshape(OWNERS, 8 * CAP, 128)
    arrived = lax.all_to_all(outgoing, "col", split_axis=0, concat_axis=0, tiled=True)
    return inverse(arrived)


def solution(mesh):
    in_specs = (
        P(("row", "col"), None, None),
        P(),
        P(("row", "col")),
        P(("row", "col")),
        P(("row", "col"), None),
    )
    out_specs = P(("row", "col"), None)
    return jax.shard_map(body, mesh=mesh, in_specs=in_specs, out_specs=out_specs, check_vma=False)
```

```python
import functools
import math

import jax
import jax.numpy as jnp
import ml_dtypes
import numpy as np
from jax import lax
from jax.experimental import pallas as pl
from jax.experimental.pallas import tpu as pltpu
from jax.sharding import PartitionSpec as P

L = 2048
BINS = 512
LOW_BIN = 8
STA = 128
CAP = 96
SIDE = 4
OWNERS = 16
PAIRS = 1024
HALF_ROWS = STA * 16 // 2

EVEN = np.arange(0, BINS, 2)
ODD = np.arange(1, BINS, 2)


def forward_tables():
    t = np.arange(L)[:, None]
    k = LOW_BIN + np.arange(BINS)[None, :]
    phase = (t * k % L) * (2.0 * math.pi / L)
    re = np.cos(phase) / math.sqrt(L)
    im = -np.sin(phase) / math.sqrt(L)
    steps = []
    for g in range(2):
        e, o = EVEN[g * 128 : (g + 1) * 128], ODD[g * 128 : (g + 1) * 128]
        steps.append(np.concatenate([re[:, e], re[:, o], im[:, e], im[:, o]], 1))
    return np.stack(steps).astype(np.float32).astype(ml_dtypes.bfloat16)


def inverse_tables():
    t = np.arange(L // 2)[None, :]
    k = LOW_BIN + np.arange(BINS)[:, None]
    phase = (t * k % L) * (2.0 * math.pi / L)
    re = np.cos(phase) / math.sqrt(BINS)
    im = -np.sin(phase) / math.sqrt(BINS)
    even = np.concatenate([re[EVEN], im[EVEN]], 0)
    odd = np.concatenate([re[ODD], im[ODD]], 0)
    return np.stack([even, odd]).astype(np.float32).astype(ml_dtypes.bfloat16)


def whiten_kernel(x_hbm, table_hbm, first_ref, second_ref, whole_ref, x_ref, table_ref, wide_ref, rows_ref, sems):
    load_x = pltpu.make_async_copy(x_hbm, x_ref, sems.at[0])
    load_x.start()
    loads = []
    for g in range(2):
        for h in range(2):
            at = pl.ds(h * (L // 2), L // 2)
            load = pltpu.make_async_copy(
                table_hbm.at[g, at, :], table_ref.at[g, at, :], sems.at[1 + 2 * g + h]
            )
            load.start()
            loads.append(load)
    load_x.wait()
    wide_ref[...] = x_ref[...].astype(jnp.float32)
    records = []
    for segment in range(2):
        blocks = [
            wide_ref[pl.ds(2 * i + segment, STA, stride=32), :].astype(jnp.bfloat16)
            for i in range(L // 128)
        ]
        records.append(jnp.concatenate(blocks, 1))
    x = jnp.concatenate(records, 0)
    lane_r = lax.broadcasted_iota(jnp.int32, (128, 128), 0)
    lane_c = lax.broadcasted_iota(jnp.int32, (128, 128), 1)
    group = jnp.where((lane_r >> 5) == (lane_c >> 5), 1.0 / 64.0, 0.0).astype(jnp.bfloat16)
    for g in range(2):
        loads[2 * g].wait()
        loads[2 * g + 1].wait()
        spectrum = jnp.dot(x, table_ref[g], preferred_element_type=jnp.float32)
        parts = [spectrum[:, i * 128 : (i + 1) * 128] for i in range(4)]
        power = sum(p * p for p in parts)
        coarse = power.astype(jnp.bfloat16)
        fine = (power - coarse.astype(jnp.float32)).astype(jnp.bfloat16)
        mean = jnp.dot(coarse, group, preferred_element_type=jnp.float32)
        mean += jnp.dot(fine, group, preferred_element_type=jnp.float32)
        scaling = lax.rsqrt(mean + 1e-06)
        for i, p in enumerate(parts):
            value = p * scaling
            for segment in range(2):
                rows_ref[pl.ds(8 * segment + 2 * i + g, STA, stride=16), :] = value[
                    segment * STA : (segment + 1) * STA
                ]
    whole = rows_ref[...].astype(jnp.bfloat16)
    first_ref[...] = whole[:HALF_ROWS]
    second_ref[...] = whole[HALF_ROWS:]
    whole_ref[...] = whole


def whiten(traces):
    half = jax.ShapeDtypeStruct((HALF_ROWS, 128), jnp.bfloat16)
    whole = jax.ShapeDtypeStruct((2 * HALF_ROWS, 128), jnp.bfloat16)
    rows = traces.reshape(STA, 2, L // 128, 128).transpose(0, 2, 1, 3).reshape(32 * STA, 128)
    vmem = pl.BlockSpec(memory_space=pltpu.VMEM)
    return pl.pallas_call(
        whiten_kernel,
        out_shape=(half, half, whole),
        in_specs=[pl.BlockSpec(memory_space=pl.ANY)] * 2,
        out_specs=(vmem, vmem, vmem),
        scratch_shapes=[
            pltpu.VMEM((32 * STA, 128), jnp.bfloat16),
            pltpu.VMEM((2, L, 512), jnp.bfloat16),
            pltpu.VMEM((32 * STA, 128), jnp.float32),
            pltpu.VMEM((2 * HALF_ROWS, 128), jnp.float32),
            pltpu.SemaphoreType.DMA((5,)),
        ],
        compiler_params=pltpu.CompilerParams(vmem_limit_bytes=55 * 1024 * 1024),
        cost_estimate=pl.CostEstimate(
            flops=2 * 256 * L * 1024, bytes_accessed=6 * 2**20, transcendentals=0
        ),
        name="whiten",
    )(rows, jnp.asarray(forward_tables()))


VMEM = pl.BlockSpec(memory_space=pltpu.VMEM)
SMEM = pl.BlockSpec(memory_space=pltpu.SMEM)


def join_kernel(counts, *refs):
    pieces, outs, sems = refs[: sum(counts)], refs[sum(counts) : -1], refs[-1]
    piece = iter(pieces)
    copies, moves = [], []
    for g, (count, out) in enumerate(zip(counts, outs)):
        at = 0
        for i in range(count):
            ref = next(piece)
            rows = ref.shape[0]
            if i == 0:
                copies.append(pltpu.make_async_copy(ref, out.at[pl.ds(at, rows), :], sems.at[g]))
                copies[-1].start()
            else:
                moves.append((out, at, ref))
            at += rows
    for out, at, ref in moves:
        out[at : at + ref.shape[0]] = ref[...]
    for copy in copies:
        copy.wait()


def join(*groups, cost=None):
    counts = tuple(len(group) for group in groups)
    shapes = [
        jax.ShapeDtypeStruct((sum(piece.shape[0] for piece in group), 128), jnp.bfloat16)
        for group in groups
    ]
    size = 256 * sum(shape.shape[0] for shape in shapes)
    return pl.pallas_call(
        functools.partial(join_kernel, counts),
        out_shape=shapes,
        in_specs=[
            pl.BlockSpec(memory_space=pl.ANY if i == 0 else pltpu.VMEM)
            for count in counts
            for i in range(count)
        ],
        out_specs=[VMEM] * len(groups),
        scratch_shapes=[pltpu.SemaphoreType.DMA((len(groups),))],
        compiler_params=pltpu.CompilerParams(vmem_limit_bytes=2 * 1024 * 1024),
        cost_estimate=pl.CostEstimate(flops=0, bytes_accessed=cost or 2 * size, transcendentals=0),
        name="join",
    )(*(piece for group in groups for piece in group))


def halves_kernel(a_ref, b_ref, c_ref, d_ref, *outs):
    rows = outs[0].shape[0]
    for ref, out in zip((a_ref, b_ref), outs[:2]):
        out[...] = ref[:rows]
    for ref, out in zip((c_ref, d_ref), outs[2:]):
        out[...] = ref[rows:]


def halves(a, b, c, d):
    half = jax.ShapeDtypeStruct((a.shape[0] // 2, 128), jnp.bfloat16)
    return pl.pallas_call(
        halves_kernel,
        out_shape=[half] * 4,
        in_specs=[VMEM] * 4,
        out_specs=[VMEM] * 4,
        compiler_params=pltpu.CompilerParams(vmem_limit_bytes=2 * 1024 * 1024),
        cost_estimate=pl.CostEstimate(
            flops=0, bytes_accessed=4 * a.shape[0] * 256, transcendentals=0
        ),
        name="halves",
    )(a, b, c, d)


def half_kernel(high, ref, out):
    rows = out.shape[0]
    out[...] = ref[rows:] if high else ref[:rows]


def half(value, high):
    return pl.pallas_call(
        functools.partial(half_kernel, high),
        out_shape=jax.ShapeDtypeStruct((value.shape[0] // 2, 128), jnp.bfloat16),
        in_specs=[VMEM],
        out_specs=VMEM,
        compiler_params=pltpu.CompilerParams(vmem_limit_bytes=2 * 1024 * 1024),
        cost_estimate=pl.CostEstimate(
            flops=0, bytes_accessed=value.shape[0] * 256, transcendentals=0
        ),
        name="half",
    )(value)


def shift(value, axis, step):
    pairs = []
    for z in range(SIDE):
        for y in range(SIDE):
            to = (z * SIDE + (y + step) % SIDE) if axis == "y" else ((z + step) % SIDE) * SIDE + y
            pairs.append((z * SIDE + y, to))
    return lax.ppermute(value, "col", pairs)


def shift_x(value, step):
    pairs = [(2 * x + k, 2 * ((x + step) % SIDE) + k) for x in range(SIDE) for k in range(2)]
    return lax.ppermute(value, "row", pairs)


def swap_cores(value):
    return lax.ppermute(value, "row", [(i, i ^ 1) for i in range(2 * SIDE)])


def ring_place(away):
    return jnp.where(away == 0, 0, jnp.where(away == 3, 1, away + 1))


def plan_kernel(first_ref, second_ref, owner_ref, taper_ref, a_ref, b_ref, slot_ref, weight_ref):
    me, row = lax.axis_index("col"), lax.axis_index("row")
    station = first_ref[...]
    home, local = station >> 7, station & 127
    place_z = ring_place(((home >> 2) - (me >> 2)) & 3)
    place_y = ring_place(((home & 3) - (me & 3)) & 3)
    over_y = jnp.where(place_z < 3, place_z * SIDE + place_y, 24 + place_y)
    over_z = jnp.where(place_y < 3, 12 + place_y * SIDE + place_z, 28 + place_z)
    block = jnp.where(local < 64, over_y, over_z)
    a_ref[...] = block * 64 + (local & 63)

    station = second_ref[...]
    home = station >> 7
    place_x = ring_place(((home >> 1) - (row >> 1)) & 3)
    b_ref[...] = (((home ^ row) & 1) * SIDE + place_x) * STA + (station & 127)

    owner = owner_ref[...]
    named = lax.broadcasted_iota(jnp.int32, (OWNERS, PAIRS), 0) == owner
    before = lax.broadcasted_iota(jnp.int32, (PAIRS, PAIRS), 0) < lax.broadcasted_iota(
        jnp.int32, (PAIRS, PAIRS), 1
    )
    counts = jnp.dot(
        jnp.where(named, 1.0, 0.0).astype(jnp.bfloat16),
        jnp.where(before, 1.0, 0.0).astype(jnp.bfloat16),
        preferred_element_type=jnp.float32,
    )
    rank = jnp.sum(jnp.where(named, counts, 0.0), axis=0, keepdims=True).astype(jnp.int32)
    slot_ref[...] = owner * (8 * CAP) + rank

    taper = taper_ref[...]
    lane = lax.broadcasted_iota(jnp.int32, (128, 128), 0)
    at = 2 * lax.broadcasted_iota(jnp.int32, (128, 128), 1)
    picked = []
    for odd in range(2):
        low, high = [
            jnp.dot(
                taper,
                jnp.where(lane + offset == at + odd, 1.0, 0.0).astype(jnp.float32),
                preferred_element_type=jnp.float32,
                precision=lax.Precision.HIGHEST,
            )
            for offset in (0, 128)
        ]
        picked += [low[0:1] + high[1:2], low[2:3] + high[3:4]]
    weight_ref[...] = jnp.concatenate(picked + picked, 0)


def plan(pair_first, pair_second, pair_owner, band_taper):
    line = jax.ShapeDtypeStruct((1, PAIRS), jnp.int32)
    return pl.pallas_call(
        plan_kernel,
        out_shape=[line, line, line, jax.ShapeDtypeStruct((8, 128), jnp.float32)],
        in_specs=[VMEM] * 4,
        out_specs=[VMEM] * 4,
        compiler_params=pltpu.CompilerParams(vmem_limit_bytes=12 * 1024 * 1024),
        cost_estimate=pl.CostEstimate(flops=2**25, bytes_accessed=2**15, transcendentals=0),
        name="plan",
    )(
        pair_first.reshape(1, PAIRS),
        pair_second.reshape(1, PAIRS),
        pair_owner.reshape(1, PAIRS),
        band_taper.reshape(4, 128),
    )


def cross_kernel(first_ref, second_ref, slot_ref, taper_ref, *refs):
    out_ref, a_ref, b_ref, cross_ref = refs[15:]
    for whole_ref, pieces in ((a_ref, refs[:7]), (b_ref, refs[7:15])):
        at = 0
        for piece in pieces:
            stations = piece.shape[0] // 16
            whole_ref[at : at + stations] = piece[...].reshape(stations, 16, 128)
            at += stations
    cross_ref[...] = jnp.zeros_like(cross_ref)
    taper = taper_ref[...]
    low = lax.broadcasted_iota(jnp.int32, (8, 128), 0) < 4
    signed = jnp.where(low, taper, -taper)
    unroll = 32

    def value(p):
        a = a_ref[first_ref[0, p]].astype(jnp.float32)
        b = b_ref[second_ref[0, p]].astype(jnp.float32)
        a0, a1, b0, b1 = a[:8], a[8:], b[:8], b[8:]
        same = a0 * b0 + a1 * b1
        swapped = a0 * pltpu.roll(b0, 4, 0) + a1 * pltpu.roll(b1, 4, 0)
        keep = jnp.where(low, same, swapped)
        move = jnp.where(low, swapped, same)
        return keep * signed + pltpu.roll(move, 4, 0) * taper

    def step(i, carry):
        for u in range(unroll):
            p = i * unroll + u
            cross_ref[pl.ds(slot_ref[0, p], 8, stride=CAP), :] = value(p)
        return carry

    lax.fori_loop(0, PAIRS // unroll, step, 0)
    out_ref[...] = cross_ref[...].astype(jnp.bfloat16)


def cross_rows(first, second, slot, taper, a_pieces, b_pieces):
    rows = OWNERS * CAP * 8
    return pl.pallas_call(
        cross_kernel,
        out_shape=jax.ShapeDtypeStruct((rows, 128), jnp.bfloat16),
        in_specs=[SMEM] * 3 + [VMEM] * 16,
        out_specs=VMEM,
        scratch_shapes=[
            pltpu.VMEM((2048, 16, 128), jnp.bfloat16),
            pltpu.VMEM((1024, 16, 128), jnp.bfloat16),
            pltpu.VMEM((rows, 128), jnp.float32),
        ],
        compiler_params=pltpu.CompilerParams(vmem_limit_bytes=20 * 1024 * 1024),
        cost_estimate=pl.CostEstimate(
            flops=16 * 1024 * 1024, bytes_accessed=15 * 2**20, transcendentals=0
        ),
        name="cross",
    )(first, second, slot, taper, *a_pieces, *b_pieces)


def inverse_kernel(cross_ref, table_ref, out_hbm, even_ref, odd_ref, lags_ref, sems):
    for s in range(OWNERS):
        rows = pl.ds(s * CAP, CAP)
        for to, columns in ((even_ref, (0, 1, 4, 5)), (odd_ref, (2, 3, 6, 7))):
            for i, j in enumerate(columns):
                to[rows, i * 128 : (i + 1) * 128] = cross_ref[s, j * CAP : (j + 1) * CAP, :]
    width = 256
    copies = []
    for n in range(0, L // 2, width):
        e = jnp.dot(
            even_ref[...], table_ref[0, :, n : n + width], preferred_element_type=jnp.float32
        )
        o = jnp.dot(
            odd_ref[...], table_ref[1, :, n : n + width], preferred_element_type=jnp.float32
        )
        for at, lags in ((n, e + o), (L // 2 + n, e - o)):
            columns = pl.ds(at, width)
            lags_ref[:, columns] = lags.astype(jnp.bfloat16)
            copies.append(
                pltpu.make_async_copy(
                    lags_ref.at[:, columns], out_hbm.at[:, columns], sems.at[len(copies)]
                )
            )
            copies[-1].start()
    for copy in copies:
        copy.wait()


def inverse(arrived):
    return pl.pallas_call(
        inverse_kernel,
        out_shape=jax.ShapeDtypeStruct((OWNERS * CAP, L), jnp.bfloat16),
        in_specs=[VMEM] * 2,
        out_specs=pl.BlockSpec(memory_space=pl.ANY),
        scratch_shapes=[
            pltpu.VMEM((OWNERS * CAP, BINS), jnp.bfloat16),
            pltpu.VMEM((OWNERS * CAP, BINS), jnp.bfloat16),
            pltpu.VMEM((OWNERS * CAP, L), jnp.bfloat16),
            pltpu.SemaphoreType.DMA((8,)),
        ],
        compiler_params=pltpu.CompilerParams(vmem_limit_bytes=40 * 1024 * 1024),
        cost_estimate=pl.CostEstimate(
            flops=2 * 1536 * 1024 * 1024, bytes_accessed=11 * 2**20, transcendentals=0
        ),
        name="inverse",
    )(arrived, jnp.asarray(inverse_tables()))


def body(traces, band_taper, pair_first, pair_second, pair_owner):
    first, second, slot, taper = plan(pair_first, pair_second, pair_owner, band_taper)
    first_half, second_half, whole = whiten(traces)

    together = lax.optimization_barrier
    before_y, after_y = shift(first_half, "y", 1), shift(first_half, "y", -1)
    before_z, after_z = shift(second_half, "z", 1), shift(second_half, "z", -1)
    before_x = shift_x(whole, 1)
    own_y, own_z = join([first_half], [second_half])
    before_y, own_y, own_z = together((before_y, own_y, own_z))

    low_y, low_z, high_y, high_z = halves(before_y, before_z, after_y, after_z)
    far_y = [shift(low_y, "y", 1), shift(high_y, "y", -1)]
    far_z = [shift(low_z, "z", 1), shift(high_z, "z", -1)]
    over_y, over_z = join([own_y, before_y, after_y, *far_y], [own_z, before_z, after_z, *far_z])

    before_y, after_y = shift(over_y, "z", 1), shift(over_y, "z", -1)
    before_z, after_z = shift(over_z, "y", 1), shift(over_z, "y", -1)
    from_here, before_x, _ = together((whole, before_x, over_y))
    after_x = shift_x(from_here, -1)
    from_here, after_x = together((from_here, after_x))
    far_x = shift_x(from_here, 2)

    onward = [half(before_y, 0), half(after_y, 1), half(before_z, 0), half(after_z, 1)]
    late = [shift(onward[0], "z", 1), shift(onward[1], "z", -1)]
    late += [shift(onward[2], "y", 1), shift(onward[3], "y", -1)]
    own_core = [whole, before_x, after_x, far_x]
    ready = together((*own_core, *onward))[:4]
    b_pieces = own_core + [swap_cores(block) for block in ready]
    a_pieces = [over_y, before_y, after_y, over_z, before_z, after_z]
    a_pieces += list(join(late, cost=2**26))

    cross = cross_rows(first, second, slot, taper, a_pieces, b_pieces)
    outgoing = cross.reshape(OWNERS, 8 * CAP, 128)
    arrived = lax.all_to_all(outgoing, "col", split_axis=0, concat_axis=0, tiled=True)
    return inverse(arrived)


def solution(mesh):
    in_specs = (
        P(("row", "col"), None, None),
        P(),
        P(("row", "col")),
        P(("row", "col")),
        P(("row", "col"), None),
    )
    out_specs = P(("row", "col"), None)
    return jax.shard_map(body, mesh=mesh, in_specs=in_specs, out_specs=out_specs, check_vma=False)
```

```python
import functools
import math

import jax
import jax.numpy as jnp
import ml_dtypes
import numpy as np
from jax import lax
from jax.experimental import pallas as pl
from jax.experimental.pallas import tpu as pltpu
from jax.sharding import PartitionSpec as P

L = 2048
BINS = 512
LOW_BIN = 8
STA = 128
CAP = 96
SIDE = 4
OWNERS = 16
PAIRS = 1024
CHUNKS = 4
BLOCK = STA * 16
HALF = BLOCK // 2
QUARTER = BLOCK // 4

VMEM = pl.BlockSpec(memory_space=pltpu.VMEM)
SMEM = pl.BlockSpec(memory_space=pltpu.SMEM)

EVEN = np.arange(0, BINS, 2)
ODD = np.arange(1, BINS, 2)


def forward_tables():
    t = np.arange(L)[:, None]
    k = LOW_BIN + np.arange(BINS)[None, :]
    phase = (t * k % L) * (2.0 * math.pi / L)
    re = np.cos(phase) / math.sqrt(L)
    im = -np.sin(phase) / math.sqrt(L)
    columns = []
    for g in range(2):
        e, o = EVEN[g * 128 : (g + 1) * 128], ODD[g * 128 : (g + 1) * 128]
        columns += [re[:, e], re[:, o], im[:, e], im[:, o]]
    table = np.concatenate(columns, 1).reshape(CHUNKS, L // CHUNKS, 2 * BINS)
    return table.astype(np.float32).astype(ml_dtypes.bfloat16)


def inverse_tables():
    t = np.arange(L // 2)[None, :]
    k = LOW_BIN + np.arange(BINS)[:, None]
    phase = (t * k % L) * (2.0 * math.pi / L)
    re = np.cos(phase) / math.sqrt(BINS)
    im = -np.sin(phase) / math.sqrt(BINS)
    even = np.concatenate([re[EVEN], im[EVEN]], 0)
    odd = np.concatenate([re[ODD], im[ODD]], 0)
    return np.stack([even, odd]).astype(np.float32).astype(ml_dtypes.bfloat16)


def whiten_kernel(x_hbm, table_hbm, out_ref, x_ref, table_ref, wide_ref, rows_ref, sems):
    load_x = pltpu.make_async_copy(x_hbm, x_ref, sems.at[0])
    load_x.start()
    loads = []
    for k in range(CHUNKS):
        load = pltpu.make_async_copy(table_hbm.at[k], table_ref.at[k], sems.at[1 + k])
        load.start()
        loads.append(load)
    load_x.wait()
    wide_ref[...] = x_ref[...].astype(jnp.float32)
    spectrum = None
    for k in range(CHUNKS):
        records = []
        for segment in range(2):
            blocks = [
                wide_ref[pl.ds(2 * i + segment, STA, stride=32), :].astype(jnp.bfloat16)
                for i in range(16 // CHUNKS * k, 16 // CHUNKS * (k + 1))
            ]
            records.append(jnp.concatenate(blocks, 1))
        x = jnp.concatenate(records, 0)
        loads[k].wait()
        part = jnp.dot(x, table_ref[k], preferred_element_type=jnp.float32)
        spectrum = part if k == 0 else spectrum + part
    lane_r = lax.broadcasted_iota(jnp.int32, (128, 128), 0)
    lane_c = lax.broadcasted_iota(jnp.int32, (128, 128), 1)
    group = jnp.where((lane_r >> 5) == (lane_c >> 5), 1.0 / 64.0, 0.0).astype(jnp.bfloat16)
    for g in range(2):
        parts = [spectrum[:, (4 * g + i) * 128 : (4 * g + i + 1) * 128] for i in range(4)]
        power = sum(p * p for p in parts)
        coarse = power.astype(jnp.bfloat16)
        fine = (power - coarse.astype(jnp.float32)).astype(jnp.bfloat16)
        mean = jnp.dot(coarse, group, preferred_element_type=jnp.float32)
        mean += jnp.dot(fine, group, preferred_element_type=jnp.float32)
        scaling = lax.rsqrt(mean + 1e-06)
        for i, p in enumerate(parts):
            value = p * scaling
            for segment in range(2):
                rows_ref[pl.ds(8 * segment + 2 * i + g, STA, stride=16), :] = value[
                    segment * STA : (segment + 1) * STA
                ]
    out_ref[...] = rows_ref[...].astype(jnp.bfloat16)


def whiten(traces):
    rows = traces.reshape(STA, 2, L // 128, 128).transpose(0, 2, 1, 3).reshape(32 * STA, 128)
    return pl.pallas_call(
        whiten_kernel,
        out_shape=jax.ShapeDtypeStruct((BLOCK, 128), jnp.bfloat16),
        in_specs=[pl.BlockSpec(memory_space=pl.ANY)] * 2,
        out_specs=VMEM,
        scratch_shapes=[
            pltpu.VMEM((32 * STA, 128), jnp.bfloat16),
            pltpu.VMEM((CHUNKS, L // CHUNKS, 2 * BINS), jnp.bfloat16),
            pltpu.VMEM((32 * STA, 128), jnp.float32),
            pltpu.VMEM((BLOCK, 128), jnp.float32),
            pltpu.SemaphoreType.DMA((1 + CHUNKS,)),
        ],
        compiler_params=pltpu.CompilerParams(vmem_limit_bytes=55 * 1024 * 1024),
        cost_estimate=pl.CostEstimate(
            flops=2 * 256 * L * 1024, bytes_accessed=6 * 2**20, transcendentals=0
        ),
        name="whiten",
    )(rows, jnp.asarray(forward_tables()))


def pack_kernel(plans, count, *refs):
    for plan, out in zip(plans, refs[count:]):
        at = 0
        for source, start, rows in plan:
            out[at : at + rows] = refs[source][start : start + rows]
            at += rows


def pack(sources, *plans):
    shapes = [
        jax.ShapeDtypeStruct((sum(rows for _, _, rows in plan), 128), jnp.bfloat16)
        for plan in plans
    ]
    size = 256 * sum(shape.shape[0] for shape in shapes)
    return pl.pallas_call(
        functools.partial(pack_kernel, plans, len(sources)),
        out_shape=shapes,
        in_specs=[VMEM] * len(sources),
        out_specs=[VMEM] * len(shapes),
        compiler_params=pltpu.CompilerParams(vmem_limit_bytes=2 * 1024 * 1024),
        cost_estimate=pl.CostEstimate(flops=0, bytes_accessed=2 * size, transcendentals=0),
        name="pack",
    )(*sources)


def shift(value, axis, step):
    pairs = []
    for z in range(SIDE):
        for y in range(SIDE):
            to = (z * SIDE + (y + step) % SIDE) if axis == "y" else ((z + step) % SIDE) * SIDE + y
            pairs.append((z * SIDE + y, to))
    return lax.ppermute(value, "col", pairs)


def shift_x(value, step):
    pairs = [(2 * x + k, 2 * ((x + step) % SIDE) + k) for x in range(SIDE) for k in range(2)]
    return lax.ppermute(value, "row", pairs)


def swap_cores(value):
    return lax.ppermute(value, "row", [(i, i ^ 1) for i in range(2 * SIDE)])


def ring_place(away):
    return jnp.where(away == 0, 0, jnp.where(away == 3, 1, away + 1))


def plan_kernel(first_ref, second_ref, owner_ref, taper_ref, a_ref, b_ref, slot_ref, weight_ref):
    me, row = lax.axis_index("col"), lax.axis_index("row")
    station = first_ref[...]
    home, local = station >> 7, station & 127
    place_z = ring_place(((home >> 2) - (me >> 2)) & 3)
    place_y = ring_place(((home & 3) - (me & 3)) & 3)
    over_y = jnp.where(place_y == 0, place_z, 3 + 3 * place_z + place_y)
    over_z = jnp.where(place_z == 0, place_y, 3 + 3 * place_y + place_z)
    a_ref[...] = jnp.where(local < 64, over_y, 16 + over_z) * 64 + (local & 63)

    station = second_ref[...]
    home = station >> 7
    place_x = ring_place(((home >> 1) - (row >> 1)) & 3)
    b_ref[...] = (((home ^ row) & 1) * SIDE + place_x) * STA + (station & 127)

    owner = owner_ref[...]
    named = lax.broadcasted_iota(jnp.int32, (OWNERS, PAIRS), 0) == owner
    before = lax.broadcasted_iota(jnp.int32, (PAIRS, PAIRS), 0) < lax.broadcasted_iota(
        jnp.int32, (PAIRS, PAIRS), 1
    )
    counts = jnp.dot(
        jnp.where(named, 1.0, 0.0).astype(jnp.bfloat16),
        jnp.where(before, 1.0, 0.0).astype(jnp.bfloat16),
        preferred_element_type=jnp.float32,
    )
    rank = jnp.sum(jnp.where(named, counts, 0.0), axis=0, keepdims=True).astype(jnp.int32)
    slot_ref[...] = owner * (8 * CAP) + rank

    taper = taper_ref[...]
    lane = lax.broadcasted_iota(jnp.int32, (128, 128), 0)
    at = 2 * lax.broadcasted_iota(jnp.int32, (128, 128), 1)
    picked = []
    for odd in range(2):
        low, high = [
            jnp.dot(
                taper,
                jnp.where(lane + offset == at + odd, 1.0, 0.0).astype(jnp.float32),
                preferred_element_type=jnp.float32,
                precision=lax.Precision.HIGHEST,
            )
            for offset in (0, 128)
        ]
        picked += [low[0:1] + high[1:2], low[2:3] + high[3:4]]
    weight_ref[...] = jnp.concatenate(picked + picked, 0)


def plan(pair_first, pair_second, pair_owner, band_taper):
    line = jax.ShapeDtypeStruct((1, PAIRS), jnp.int32)
    return pl.pallas_call(
        plan_kernel,
        out_shape=[line, line, line, jax.ShapeDtypeStruct((8, 128), jnp.float32)],
        in_specs=[VMEM] * 4,
        out_specs=[VMEM] * 4,
        compiler_params=pltpu.CompilerParams(vmem_limit_bytes=12 * 1024 * 1024),
        cost_estimate=pl.CostEstimate(flops=2**25, bytes_accessed=2**15, transcendentals=0),
        name="plan",
    )(
        pair_first.reshape(1, PAIRS),
        pair_second.reshape(1, PAIRS),
        pair_owner.reshape(1, PAIRS),
        band_taper.reshape(4, 128),
    )


A_PARTS = [(0, 0, HALF), (1, 0, HALF), (2, 0, HALF)]
A_PARTS += [(8, 3 * QUARTER, QUARTER), (9, 3 * QUARTER, QUARTER)]
A_PARTS += [(7, 0, 3 * HALF), (5, 0, 3 * HALF), (6, 0, 3 * HALF)]
A_PARTS += [(8, 0, 3 * QUARTER), (9, 0, 3 * QUARTER)]
A_PARTS += [(0, HALF, HALF), (3, HALF, HALF), (4, HALF, HALF)]
A_PARTS += [(13, 3 * QUARTER, QUARTER), (14, 3 * QUARTER, QUARTER)]
A_PARTS += [(12, 0, 3 * HALF), (10, 0, 3 * HALF), (11, 0, 3 * HALF)]
A_PARTS += [(13, 0, 3 * QUARTER), (14, 0, 3 * QUARTER)]
B_PARTS = [(i, 0, BLOCK) for i in (0, 15, 16, 17, 18, 19, 20, 21)]


def cross_kernel(first_ref, second_ref, slot_ref, taper_ref, *refs):
    out_ref, a_ref, b_ref, cross_ref = refs[22:]
    for whole_ref, parts in ((a_ref, A_PARTS), (b_ref, B_PARTS)):
        at = 0
        for piece, start, rows in parts:
            stations = rows // 16
            block = refs[piece][start : start + rows].reshape(stations, 16, 128)
            whole_ref[at : at + stations] = block
            at += stations
    cross_ref[...] = jnp.zeros_like(cross_ref)
    taper = taper_ref[...]
    low = lax.broadcasted_iota(jnp.int32, (8, 128), 0) < 4
    signed = jnp.where(low, taper, -taper)
    unroll = 64

    def value(p):
        a = a_ref[first_ref[0, p]].astype(jnp.float32)
        b = b_ref[second_ref[0, p]].astype(jnp.float32)
        a0, a1, b0, b1 = a[:8], a[8:], b[:8], b[8:]
        same = a0 * b0 + a1 * b1
        swapped = a0 * pltpu.roll(b0, 4, 0) + a1 * pltpu.roll(b1, 4, 0)
        keep = jnp.where(low, same, swapped)
        move = jnp.where(low, swapped, same)
        return keep * signed + pltpu.roll(move, 4, 0) * taper

    def step(i, carry):
        for u in range(unroll):
            p = i * unroll + u
            cross_ref[pl.ds(slot_ref[0, p], 8, stride=CAP), :] = value(p)
        return carry

    lax.fori_loop(0, PAIRS // unroll, step, 0)
    out_ref[...] = cross_ref[...].astype(jnp.bfloat16)


def cross_rows(first, second, slot, taper, a_pieces, b_pieces):
    rows = OWNERS * CAP * 8
    return pl.pallas_call(
        cross_kernel,
        out_shape=jax.ShapeDtypeStruct((rows, 128), jnp.bfloat16),
        in_specs=[SMEM] * 3 + [VMEM] * 23,
        out_specs=VMEM,
        scratch_shapes=[
            pltpu.VMEM((2048, 16, 128), jnp.bfloat16),
            pltpu.VMEM((1024, 16, 128), jnp.bfloat16),
            pltpu.VMEM((rows, 128), jnp.float32),
        ],
        compiler_params=pltpu.CompilerParams(vmem_limit_bytes=20 * 1024 * 1024),
        cost_estimate=pl.CostEstimate(
            flops=16 * 1024 * 1024, bytes_accessed=15 * 2**20, transcendentals=0
        ),
        name="cross",
    )(first, second, slot, taper, *a_pieces, *b_pieces)


def inverse_kernel(cross_ref, table_ref, out_hbm, even_ref, odd_ref, lags_ref, sems):
    for s in range(OWNERS):
        rows = pl.ds(s * CAP, CAP)
        for to, columns in ((even_ref, (0, 1, 4, 5)), (odd_ref, (2, 3, 6, 7))):
            for i, j in enumerate(columns):
                to[rows, i * 128 : (i + 1) * 128] = cross_ref[s, j * CAP : (j + 1) * CAP, :]
    width = 256
    copies = []
    for n in range(0, L // 2, width):
        e = jnp.dot(
            even_ref[...], table_ref[0, :, n : n + width], preferred_element_type=jnp.float32
        )
        o = jnp.dot(
            odd_ref[...], table_ref[1, :, n : n + width], preferred_element_type=jnp.float32
        )
        for at, lags in ((n, e + o), (L // 2 + n, e - o)):
            columns = pl.ds(at, width)
            lags_ref[:, columns] = lags.astype(jnp.bfloat16)
            copies.append(
                pltpu.make_async_copy(
                    lags_ref.at[:, columns], out_hbm.at[:, columns], sems.at[len(copies)]
                )
            )
            copies[-1].start()
    for copy in copies:
        copy.wait()


def inverse(arrived):
    return pl.pallas_call(
        inverse_kernel,
        out_shape=jax.ShapeDtypeStruct((OWNERS * CAP, L), jnp.bfloat16),
        in_specs=[VMEM] * 2,
        out_specs=pl.BlockSpec(memory_space=pl.ANY),
        scratch_shapes=[
            pltpu.VMEM((OWNERS * CAP, BINS), jnp.bfloat16),
            pltpu.VMEM((OWNERS * CAP, BINS), jnp.bfloat16),
            pltpu.VMEM((OWNERS * CAP, L), jnp.bfloat16),
            pltpu.SemaphoreType.DMA((8,)),
        ],
        compiler_params=pltpu.CompilerParams(vmem_limit_bytes=40 * 1024 * 1024),
        cost_estimate=pl.CostEstimate(
            flops=2 * 1536 * 1024 * 1024, bytes_accessed=11 * 2**20, transcendentals=0
        ),
        name="inverse",
    )(arrived, jnp.asarray(inverse_tables()))


def body(traces, band_taper, pair_first, pair_second, pair_owner):
    first, second, slot, taper = plan(pair_first, pair_second, pair_owner, band_taper)
    whole = whiten(traces)

    together = lax.optimization_barrier
    y_before, y_after = shift(whole, "y", 1), shift(whole, "y", -1)
    z_before, z_after = shift(whole, "z", 1), shift(whole, "z", -1)
    before_x = shift_x(whole, 1)

    (low_y,), (high_y,) = pack([y_before], [(0, 0, QUARTER)]), pack([y_after], [(0, QUARTER, QUARTER)])
    (low_z,) = pack([z_before], [(0, HALF, QUARTER)])
    (high_z,) = pack([z_after], [(0, HALF + QUARTER, QUARTER)])
    far_y = [shift(low_y, "y", 1), shift(high_y, "y", -1)]
    far_z = [shift(low_z, "z", 1), shift(high_z, "z", -1)]

    def three(before, after, far, start):
        blocks = [(0, start, HALF), (1, start, HALF), (2, 0, QUARTER), (3, 0, QUARTER)]
        return pack([before, after, *far], blocks)[0]

    over_y, over_z = three(y_before, y_after, far_y, 0), three(z_before, z_after, far_z, HALF)
    from_z_before, from_z_after = shift(over_y, "z", 1), shift(over_y, "z", -1)
    from_y_before, from_y_after = shift(over_z, "y", 1), shift(over_z, "y", -1)
    from_here, before_x, _ = together((whole, before_x, over_y))
    after_x = shift_x(from_here, -1)
    from_here, after_x = together((from_here, after_x))
    far_x = shift_x(from_here, 2)

    def lower(three, block, start):
        return pack([three, block], [(0, 0, 3 * QUARTER), (1, start, QUARTER)])[0]

    def upper(three, block, start):
        rows = [(0, 3 * QUARTER, 3 * QUARTER), (1, start + QUARTER, QUARTER)]
        return pack([three, block], rows)[0]

    onward = [lower(from_z_before, z_before, 0), upper(from_z_after, z_after, 0)]
    onward += [lower(from_y_before, y_before, HALF), upper(from_y_after, y_after, HALF)]
    late = [shift(onward[0], "z", 1), shift(onward[1], "z", -1)]
    late += [shift(onward[2], "y", 1), shift(onward[3], "y", -1)]
    own_core = [whole, before_x, after_x, far_x]
    ready = together((*own_core, *onward))[:4]
    there = [swap_cores(block) for block in ready]
    a_pieces = [whole, z_before, z_after, y_before, y_after]
    a_pieces += [from_z_before, from_z_after, over_y, *late[:2]]
    a_pieces += [from_y_before, from_y_after, over_z, *late[2:]]
    b_pieces = [before_x, after_x, far_x, *there]

    cross = cross_rows(first, second, slot, taper, a_pieces, b_pieces)
    outgoing = cross.reshape(OWNERS, 8 * CAP, 128)
    arrived = lax.all_to_all(outgoing, "col", split_axis=0, concat_axis=0, tiled=True)
    return inverse(arrived)


def solution(mesh):
    in_specs = (
        P(("row", "col"), None, None),
        P(),
        P(("row", "col")),
        P(("row", "col")),
        P(("row", "col"), None),
    )
    out_specs = P(("row", "col"), None)
    return jax.shard_map(body, mesh=mesh, in_specs=in_specs, out_specs=out_specs, check_vma=False)
```

```python
import functools
import math

import jax
import jax.numpy as jnp
import ml_dtypes
import numpy as np
from jax import lax
from jax.experimental import pallas as pl
from jax.experimental.pallas import tpu as pltpu
from jax.sharding import PartitionSpec as P

L = 2048
BINS = 512
LOW_BIN = 8
STA = 128
CAP = 96
SIDE = 4
OWNERS = 16
PAIRS = 1024
CHUNKS = 4
BLOCK = STA * 16
HALF = BLOCK // 2
QUARTER = BLOCK // 4

VMEM = pl.BlockSpec(memory_space=pltpu.VMEM)
SMEM = pl.BlockSpec(memory_space=pltpu.SMEM)

EVEN = np.arange(0, BINS, 2)
ODD = np.arange(1, BINS, 2)


def forward_tables():
    t = np.arange(L)[:, None]
    k = LOW_BIN + np.arange(BINS)[None, :]
    phase = (t * k % L) * (2.0 * math.pi / L)
    re = np.cos(phase) / math.sqrt(L)
    im = -np.sin(phase) / math.sqrt(L)
    columns = []
    for g in range(2):
        e, o = EVEN[g * 128 : (g + 1) * 128], ODD[g * 128 : (g + 1) * 128]
        columns += [re[:, e], re[:, o], im[:, e], im[:, o]]
    table = np.concatenate(columns, 1).reshape(CHUNKS, L // CHUNKS, 2 * BINS)
    return table.astype(np.float32).astype(ml_dtypes.bfloat16)


def inverse_tables():
    t = np.arange(L // 2)[None, :]
    k = LOW_BIN + np.arange(BINS)[:, None]
    phase = (t * k % L) * (2.0 * math.pi / L)
    re = np.cos(phase) / math.sqrt(BINS)
    im = -np.sin(phase) / math.sqrt(BINS)
    even = np.concatenate([re[EVEN], im[EVEN]], 0)
    odd = np.concatenate([re[ODD], im[ODD]], 0)
    return np.stack([even, odd]).astype(np.float32).astype(ml_dtypes.bfloat16)


def whiten_kernel(x_hbm, table_hbm, out_ref, x_ref, table_ref, wide_ref, rows_ref, sems):
    load_x = pltpu.make_async_copy(x_hbm, x_ref, sems.at[0])
    load_x.start()
    loads = []
    for k in range(CHUNKS):
        load = pltpu.make_async_copy(table_hbm.at[k], table_ref.at[k], sems.at[1 + k])
        load.start()
        loads.append(load)
    load_x.wait()
    wide_ref[...] = x_ref[...].astype(jnp.float32)
    spectrum = None
    for k in range(CHUNKS):
        records = []
        for segment in range(2):
            blocks = [
                wide_ref[pl.ds(2 * i + segment, STA, stride=32), :].astype(jnp.bfloat16)
                for i in range(16 // CHUNKS * k, 16 // CHUNKS * (k + 1))
            ]
            records.append(jnp.concatenate(blocks, 1))
        x = jnp.concatenate(records, 0)
        loads[k].wait()
        part = jnp.dot(x, table_ref[k], preferred_element_type=jnp.float32)
        spectrum = part if k == 0 else spectrum + part
    lane_r = lax.broadcasted_iota(jnp.int32, (128, 128), 0)
    lane_c = lax.broadcasted_iota(jnp.int32, (128, 128), 1)
    group = jnp.where((lane_r >> 5) == (lane_c >> 5), 1.0 / 64.0, 0.0).astype(jnp.bfloat16)
    for g in range(2):
        parts = [spectrum[:, (4 * g + i) * 128 : (4 * g + i + 1) * 128] for i in range(4)]
        power = sum(p * p for p in parts)
        coarse = power.astype(jnp.bfloat16)
        fine = (power - coarse.astype(jnp.float32)).astype(jnp.bfloat16)
        mean = jnp.dot(coarse, group, preferred_element_type=jnp.float32)
        mean += jnp.dot(fine, group, preferred_element_type=jnp.float32)
        scaling = lax.rsqrt(mean + 1e-06)
        for i, p in enumerate(parts):
            value = p * scaling
            for segment in range(2):
                rows_ref[pl.ds(8 * segment + 2 * i + g, STA, stride=16), :] = value[
                    segment * STA : (segment + 1) * STA
                ]
    out_ref[...] = rows_ref[...].astype(jnp.bfloat16)


def whiten(traces):
    rows = traces.reshape(STA, 2, L // 128, 128).transpose(0, 2, 1, 3).reshape(32 * STA, 128)
    return pl.pallas_call(
        whiten_kernel,
        out_shape=jax.ShapeDtypeStruct((BLOCK, 128), jnp.bfloat16),
        in_specs=[pl.BlockSpec(memory_space=pl.ANY)] * 2,
        out_specs=VMEM,
        scratch_shapes=[
            pltpu.VMEM((32 * STA, 128), jnp.bfloat16),
            pltpu.VMEM((CHUNKS, L // CHUNKS, 2 * BINS), jnp.bfloat16),
            pltpu.VMEM((32 * STA, 128), jnp.float32),
            pltpu.VMEM((BLOCK, 128), jnp.float32),
            pltpu.SemaphoreType.DMA((1 + CHUNKS,)),
        ],
        compiler_params=pltpu.CompilerParams(vmem_limit_bytes=55 * 1024 * 1024),
        cost_estimate=pl.CostEstimate(
            flops=2 * 256 * L * 1024, bytes_accessed=6 * 2**20, transcendentals=0
        ),
        name="whiten",
    )(rows, jnp.asarray(forward_tables()))


def pack_kernel(plans, count, *refs):
    for plan, out in zip(plans, refs[count:]):
        at = 0
        for source, start, rows in plan:
            out[at : at + rows] = refs[source][start : start + rows]
            at += rows


def pack(sources, *plans):
    shapes = [
        jax.ShapeDtypeStruct((sum(rows for _, _, rows in plan), 128), jnp.bfloat16)
        for plan in plans
    ]
    size = 256 * sum(shape.shape[0] for shape in shapes)
    return pl.pallas_call(
        functools.partial(pack_kernel, plans, len(sources)),
        out_shape=shapes,
        in_specs=[VMEM] * len(sources),
        out_specs=[VMEM] * len(shapes),
        compiler_params=pltpu.CompilerParams(vmem_limit_bytes=2 * 1024 * 1024),
        cost_estimate=pl.CostEstimate(flops=0, bytes_accessed=2 * size, transcendentals=0),
        name="pack",
    )(*sources)


def shift(value, axis, step):
    pairs = []
    for z in range(SIDE):
        for y in range(SIDE):
            to = (z * SIDE + (y + step) % SIDE) if axis == "y" else ((z + step) % SIDE) * SIDE + y
            pairs.append((z * SIDE + y, to))
    return lax.ppermute(value, "col", pairs)


def shift_x(value, step):
    pairs = [(2 * x + k, 2 * ((x + step) % SIDE) + k) for x in range(SIDE) for k in range(2)]
    return lax.ppermute(value, "row", pairs)


def swap_cores(value):
    return lax.ppermute(value, "row", [(i, i ^ 1) for i in range(2 * SIDE)])


def ring_place(away):
    return jnp.where(away == 0, 0, jnp.where(away == 3, 1, away + 1))


def plan_kernel(first_ref, second_ref, owner_ref, taper_ref, a_ref, b_ref, slot_ref, weight_ref):
    me, row = lax.axis_index("col"), lax.axis_index("row")
    station = first_ref[...]
    home, local = station >> 7, station & 127
    place_z = ring_place(((home >> 2) - (me >> 2)) & 3)
    place_y = ring_place(((home & 3) - (me & 3)) & 3)
    over_y = jnp.where(place_y == 0, place_z, 3 + 3 * place_z + place_y)
    over_z = jnp.where(place_z == 0, place_y, 3 + 3 * place_y + place_z)
    a_ref[...] = jnp.where(local < 64, over_y, 16 + over_z) * 64 + (local & 63)

    station = second_ref[...]
    home = station >> 7
    place_x = ring_place(((home >> 1) - (row >> 1)) & 3)
    b_ref[...] = (((home ^ row) & 1) * SIDE + place_x) * STA + (station & 127)

    owner = owner_ref[...]
    named = lax.broadcasted_iota(jnp.int32, (OWNERS, PAIRS), 0) == owner
    before = lax.broadcasted_iota(jnp.int32, (PAIRS, PAIRS), 0) < lax.broadcasted_iota(
        jnp.int32, (PAIRS, PAIRS), 1
    )
    counts = jnp.dot(
        jnp.where(named, 1.0, 0.0).astype(jnp.bfloat16),
        jnp.where(before, 1.0, 0.0).astype(jnp.bfloat16),
        preferred_element_type=jnp.float32,
    )
    rank = jnp.sum(jnp.where(named, counts, 0.0), axis=0, keepdims=True).astype(jnp.int32)
    slot_ref[...] = owner * (8 * CAP) + rank

    taper = taper_ref[...]
    lane = lax.broadcasted_iota(jnp.int32, (128, 128), 0)
    at = 2 * lax.broadcasted_iota(jnp.int32, (128, 128), 1)
    picked = []
    for odd in range(2):
        low, high = [
            jnp.dot(
                taper,
                jnp.where(lane + offset == at + odd, 1.0, 0.0).astype(jnp.float32),
                preferred_element_type=jnp.float32,
                precision=lax.Precision.HIGHEST,
            )
            for offset in (0, 128)
        ]
        picked += [low[0:1] + high[1:2], low[2:3] + high[3:4]]
    weight_ref[...] = jnp.concatenate(picked + picked, 0)


def plan(pair_first, pair_second, pair_owner, band_taper):
    line = jax.ShapeDtypeStruct((1, PAIRS), jnp.int32)
    return pl.pallas_call(
        plan_kernel,
        out_shape=[line, line, line, jax.ShapeDtypeStruct((8, 128), jnp.float32)],
        in_specs=[VMEM] * 4,
        out_specs=[VMEM] * 4,
        compiler_params=pltpu.CompilerParams(vmem_limit_bytes=12 * 1024 * 1024),
        cost_estimate=pl.CostEstimate(flops=2**25, bytes_accessed=2**15, transcendentals=0),
        name="plan",
    )(
        pair_first.reshape(1, PAIRS),
        pair_second.reshape(1, PAIRS),
        pair_owner.reshape(1, PAIRS),
        band_taper.reshape(4, 128),
    )


A_PARTS = [(0, 0, HALF), (1, 0, HALF), (2, 0, HALF)]
A_PARTS += [(8, 3 * QUARTER, QUARTER), (9, 3 * QUARTER, QUARTER)]
A_PARTS += [(7, 0, 3 * HALF), (5, 0, 3 * HALF), (6, 0, 3 * HALF)]
A_PARTS += [(8, 0, 3 * QUARTER), (9, 0, 3 * QUARTER)]
A_PARTS += [(0, HALF, HALF), (3, HALF, HALF), (4, HALF, HALF)]
A_PARTS += [(13, 3 * QUARTER, QUARTER), (14, 3 * QUARTER, QUARTER)]
A_PARTS += [(12, 0, 3 * HALF), (10, 0, 3 * HALF), (11, 0, 3 * HALF)]
A_PARTS += [(13, 0, 3 * QUARTER), (14, 0, 3 * QUARTER)]
B_PARTS = [(i, 0, BLOCK) for i in (0, 15, 16, 17, 18, 19, 20, 21)]


def cross_kernel(first_ref, second_ref, slot_ref, taper_ref, *refs):
    out_ref, a_ref, b_ref, cross_ref = refs[22:]
    for whole_ref, parts in ((a_ref, A_PARTS), (b_ref, B_PARTS)):
        at = 0
        for piece, start, rows in parts:
            stations = rows // 16
            block = refs[piece][start : start + rows].reshape(stations, 16, 128)
            whole_ref[at : at + stations] = block
            at += stations
    cross_ref[: out_ref.shape[0]] = jnp.zeros(out_ref.shape, jnp.float32)
    taper = taper_ref[...]
    low = lax.broadcasted_iota(jnp.int32, (8, 128), 0) < 4
    signed = jnp.where(low, taper, -taper)
    unroll = 64

    def value(p):
        a = a_ref[first_ref[0, p]].astype(jnp.float32)
        b = b_ref[second_ref[0, p]].astype(jnp.float32)
        a0, a1, b0, b1 = a[:8], a[8:], b[:8], b[8:]
        same = a0 * b0 + a1 * b1
        swapped = a0 * pltpu.roll(b0, 4, 0) + a1 * pltpu.roll(b1, 4, 0)
        keep = jnp.where(low, same, swapped)
        move = jnp.where(low, swapped, same)
        return keep * signed + pltpu.roll(move, 4, 0) * taper

    def step(i, carry):
        for u in range(unroll):
            p = i * unroll + u
            cross_ref[pl.ds(slot_ref[0, p], 8, stride=CAP), :] = value(p)
        return carry

    lax.fori_loop(0, PAIRS // unroll, step, 0)
    out_ref[...] = cross_ref[: out_ref.shape[0]].astype(jnp.bfloat16)


def cross_rows(first, second, slot, taper, a_pieces, b_pieces):
    rows = OWNERS * CAP * 8
    return pl.pallas_call(
        cross_kernel,
        out_shape=jax.ShapeDtypeStruct((rows, 128), jnp.bfloat16),
        in_specs=[SMEM] * 3 + [VMEM] * 23,
        out_specs=VMEM,
        scratch_shapes=[
            pltpu.VMEM((2048, 16, 128), jnp.bfloat16),
            pltpu.VMEM((1024, 16, 128), jnp.bfloat16),
            pltpu.VMEM((rows + 8 * CAP, 128), jnp.float32),
        ],
        compiler_params=pltpu.CompilerParams(vmem_limit_bytes=20 * 1024 * 1024),
        cost_estimate=pl.CostEstimate(
            flops=16 * 1024 * 1024, bytes_accessed=15 * 2**20, transcendentals=0
        ),
        name="cross",
    )(first, second, slot, taper, *a_pieces, *b_pieces)


def inverse_kernel(cross_ref, table_ref, out_hbm, even_ref, odd_ref, lags_ref, sems):
    for s in range(OWNERS):
        rows = pl.ds(s * CAP, CAP)
        for to, columns in ((even_ref, (0, 1, 4, 5)), (odd_ref, (2, 3, 6, 7))):
            for i, j in enumerate(columns):
                to[rows, i * 128 : (i + 1) * 128] = cross_ref[s, j * CAP : (j + 1) * CAP, :]
    width = 256
    copies = []
    for n in range(0, L // 2, width):
        e = jnp.dot(
            even_ref[...], table_ref[0, :, n : n + width], preferred_element_type=jnp.float32
        )
        o = jnp.dot(
            odd_ref[...], table_ref[1, :, n : n + width], preferred_element_type=jnp.float32
        )
        for at, lags in ((n, e + o), (L // 2 + n, e - o)):
            columns = pl.ds(at, width)
            lags_ref[:, columns] = lags.astype(jnp.bfloat16)
            copies.append(
                pltpu.make_async_copy(
                    lags_ref.at[:, columns], out_hbm.at[:, columns], sems.at[len(copies)]
                )
            )
            copies[-1].start()
    for copy in copies:
        copy.wait()


def inverse(arrived):
    return pl.pallas_call(
        inverse_kernel,
        out_shape=jax.ShapeDtypeStruct((OWNERS * CAP, L), jnp.bfloat16),
        in_specs=[VMEM] * 2,
        out_specs=pl.BlockSpec(memory_space=pl.ANY),
        scratch_shapes=[
            pltpu.VMEM((OWNERS * CAP, BINS), jnp.bfloat16),
            pltpu.VMEM((OWNERS * CAP, BINS), jnp.bfloat16),
            pltpu.VMEM((OWNERS * CAP, L), jnp.bfloat16),
            pltpu.SemaphoreType.DMA((8,)),
        ],
        compiler_params=pltpu.CompilerParams(vmem_limit_bytes=40 * 1024 * 1024),
        cost_estimate=pl.CostEstimate(
            flops=2 * 1536 * 1024 * 1024, bytes_accessed=11 * 2**20, transcendentals=0
        ),
        name="inverse",
    )(arrived, jnp.asarray(inverse_tables()))


def body(traces, band_taper, pair_first, pair_second, pair_owner):
    first, second, slot, taper = plan(pair_first, pair_second, pair_owner, band_taper)
    whole = whiten(traces)

    together = lax.optimization_barrier
    y_before, y_after = shift(whole, "y", 1), shift(whole, "y", -1)
    z_before, z_after = shift(whole, "z", 1), shift(whole, "z", -1)
    before_x = shift_x(whole, 1)

    (low_y,), (high_y,) = pack([y_before], [(0, 0, QUARTER)]), pack([y_after], [(0, QUARTER, QUARTER)])
    (low_z,) = pack([z_before], [(0, HALF, QUARTER)])
    (high_z,) = pack([z_after], [(0, HALF + QUARTER, QUARTER)])
    far_y = [shift(low_y, "y", 1), shift(high_y, "y", -1)]
    far_z = [shift(low_z, "z", 1), shift(high_z, "z", -1)]

    def three(before, after, far, start):
        blocks = [(0, start, HALF), (1, start, HALF), (2, 0, QUARTER), (3, 0, QUARTER)]
        return pack([before, after, *far], blocks)[0]

    over_y, over_z = three(y_before, y_after, far_y, 0), three(z_before, z_after, far_z, HALF)
    from_z_before, from_z_after = shift(over_y, "z", 1), shift(over_y, "z", -1)
    from_y_before, from_y_after = shift(over_z, "y", 1), shift(over_z, "y", -1)
    from_here, before_x, _ = together((whole, before_x, over_y))
    after_x = shift_x(from_here, -1)
    from_here, after_x = together((from_here, after_x))
    far_x = shift_x(from_here, 2)

    def lower(three, block, start):
        return pack([three, block], [(0, 0, 3 * QUARTER), (1, start, QUARTER)])[0]

    def upper(three, block, start):
        rows = [(0, 3 * QUARTER, 3 * QUARTER), (1, start + QUARTER, QUARTER)]
        return pack([three, block], rows)[0]

    onward = [lower(from_z_before, z_before, 0), upper(from_z_after, z_after, 0)]
    onward += [lower(from_y_before, y_before, HALF), upper(from_y_after, y_after, HALF)]
    late = [shift(onward[0], "z", 1), shift(onward[1], "z", -1)]
    late += [shift(onward[2], "y", 1), shift(onward[3], "y", -1)]
    own_core = [whole, before_x, after_x, far_x]
    ready = together((*own_core, *onward))[:4]
    there = [swap_cores(block) for block in ready]
    a_pieces = [whole, z_before, z_after, y_before, y_after]
    a_pieces += [from_z_before, from_z_after, over_y, *late[:2]]
    a_pieces += [from_y_before, from_y_after, over_z, *late[2:]]
    b_pieces = [before_x, after_x, far_x, *there]

    cross = cross_rows(first, second, slot, taper, a_pieces, b_pieces)
    outgoing = cross.reshape(OWNERS, 8 * CAP, 128)
    arrived = lax.all_to_all(outgoing, "col", split_axis=0, concat_axis=0, tiled=True)
    return inverse(arrived)


def solution(mesh):
    in_specs = (
        P(("row", "col"), None, None),
        P(),
        P(("row", "col")),
        P(("row", "col")),
        P(("row", "col"), None),
    )
    out_specs = P(("row", "col"), None)
    return jax.shard_map(body, mesh=mesh, in_specs=in_specs, out_specs=out_specs, check_vma=False)
```

```python
import functools
import math

import jax
import jax.numpy as jnp
import ml_dtypes
import numpy as np
from jax import lax
from jax.experimental import pallas as pl
from jax.experimental.pallas import tpu as pltpu
from jax.sharding import PartitionSpec as P

L = 2048
BINS = 512
LOW_BIN = 8
STA = 128
CAP = 96
SIDE = 4
OWNERS = 16
PAIRS = 1024
CHUNKS = 2
BLOCK = STA * 16
HALF = BLOCK // 2
QUARTER = BLOCK // 4

VMEM = pl.BlockSpec(memory_space=pltpu.VMEM)
SMEM = pl.BlockSpec(memory_space=pltpu.SMEM)

EVEN = np.arange(0, BINS, 2)
ODD = np.arange(1, BINS, 2)


def forward_tables():
    t = np.arange(L)[:, None]
    k = LOW_BIN + np.arange(BINS)[None, :]
    phase = (t * k % L) * (2.0 * math.pi / L)
    re = np.cos(phase) / math.sqrt(L)
    im = -np.sin(phase) / math.sqrt(L)
    half = L // 2
    tables = []
    for bins in (EVEN, ODD):
        columns = []
        for g in range(2):
            chosen = bins[g * 128 : (g + 1) * 128]
            columns += [re[:half, chosen], im[:half, chosen]]
        tables.append(np.concatenate(columns, 1).reshape(CHUNKS, half // CHUNKS, BINS))
    return np.stack(tables, 1).astype(np.float32).astype(ml_dtypes.bfloat16)


def inverse_tables():
    t = np.arange(L // 2)[None, :]
    k = LOW_BIN + np.arange(BINS)[:, None]
    phase = (t * k % L) * (2.0 * math.pi / L)
    re = np.cos(phase) / math.sqrt(BINS)
    im = -np.sin(phase) / math.sqrt(BINS)
    even = np.concatenate([re[EVEN], im[EVEN]], 0)
    odd = np.concatenate([re[ODD], im[ODD]], 0)
    return np.stack([even, odd]).astype(np.float32).astype(ml_dtypes.bfloat16)


def whiten_kernel(x_hbm, table_hbm, out_ref, x_ref, table_ref, wide_ref, rows_ref, sems):
    load_x = pltpu.make_async_copy(x_hbm, x_ref, sems.at[0])
    load_x.start()
    loads = []
    for k in range(CHUNKS):
        load = pltpu.make_async_copy(table_hbm.at[k], table_ref.at[k], sems.at[1 + k])
        load.start()
        loads.append(load)
    load_x.wait()
    wide_ref[...] = x_ref[...].astype(jnp.float32)
    spectra = [None, None]
    for k in range(CHUNKS):
        sums, differences = [], []
        for segment in range(2):
            added, taken = [], []
            for i in range(8 // CHUNKS * k, 8 // CHUNKS * (k + 1)):
                first = wide_ref[pl.ds(2 * i + segment, STA, stride=32), :]
                second = wide_ref[pl.ds(2 * (i + 8) + segment, STA, stride=32), :]
                added.append((first + second).astype(jnp.bfloat16))
                taken.append((first - second).astype(jnp.bfloat16))
            sums.append(jnp.concatenate(added, 1))
            differences.append(jnp.concatenate(taken, 1))
        loads[k].wait()
        for parity, rows in enumerate((sums, differences)):
            part = jnp.dot(
                jnp.concatenate(rows, 0), table_ref[k, parity], preferred_element_type=jnp.float32
            )
            spectra[parity] = part if k == 0 else spectra[parity] + part
    lane_r = lax.broadcasted_iota(jnp.int32, (128, 128), 0)
    lane_c = lax.broadcasted_iota(jnp.int32, (128, 128), 1)
    group = jnp.where((lane_r >> 5) == (lane_c >> 5), 1.0 / 64.0, 0.0).astype(jnp.bfloat16)
    for g in range(2):
        parts = [
            spectra[parity][:, (2 * g + i) * 128 : (2 * g + i + 1) * 128]
            for i in range(2)
            for parity in range(2)
        ]
        power = sum(p * p for p in parts)
        coarse = power.astype(jnp.bfloat16)
        fine = (power - coarse.astype(jnp.float32)).astype(jnp.bfloat16)
        mean = jnp.dot(coarse, group, preferred_element_type=jnp.float32)
        mean += jnp.dot(fine, group, preferred_element_type=jnp.float32)
        scaling = lax.rsqrt(mean + 1e-06)
        for i, p in enumerate(parts):
            value = p * scaling
            for segment in range(2):
                rows_ref[pl.ds(8 * segment + 2 * i + g, STA, stride=16), :] = value[
                    segment * STA : (segment + 1) * STA
                ]
    out_ref[...] = rows_ref[...].astype(jnp.bfloat16)


def whiten(traces):
    rows = traces.reshape(STA, 2, L // 128, 128).transpose(0, 2, 1, 3).reshape(32 * STA, 128)
    return pl.pallas_call(
        whiten_kernel,
        out_shape=jax.ShapeDtypeStruct((BLOCK, 128), jnp.bfloat16),
        in_specs=[pl.BlockSpec(memory_space=pl.ANY)] * 2,
        out_specs=VMEM,
        scratch_shapes=[
            pltpu.VMEM((32 * STA, 128), jnp.bfloat16),
            pltpu.VMEM((CHUNKS, 2, L // 2 // CHUNKS, BINS), jnp.bfloat16),
            pltpu.VMEM((32 * STA, 128), jnp.float32),
            pltpu.VMEM((BLOCK, 128), jnp.float32),
            pltpu.SemaphoreType.DMA((1 + CHUNKS,)),
        ],
        compiler_params=pltpu.CompilerParams(vmem_limit_bytes=55 * 1024 * 1024),
        cost_estimate=pl.CostEstimate(
            flops=2 * 256 * L * 1024, bytes_accessed=6 * 2**20, transcendentals=0
        ),
        name="whiten",
    )(rows, jnp.asarray(forward_tables()))


def pack_kernel(plans, count, *refs):
    for plan, out in zip(plans, refs[count:]):
        at = 0
        for source, start, rows in plan:
            out[at : at + rows] = refs[source][start : start + rows]
            at += rows


def pack(sources, *plans):
    shapes = [
        jax.ShapeDtypeStruct((sum(rows for _, _, rows in plan), 128), jnp.bfloat16)
        for plan in plans
    ]
    size = 256 * sum(shape.shape[0] for shape in shapes)
    return pl.pallas_call(
        functools.partial(pack_kernel, plans, len(sources)),
        out_shape=shapes,
        in_specs=[VMEM] * len(sources),
        out_specs=[VMEM] * len(shapes),
        compiler_params=pltpu.CompilerParams(vmem_limit_bytes=2 * 1024 * 1024),
        cost_estimate=pl.CostEstimate(flops=0, bytes_accessed=2 * size, transcendentals=0),
        name="pack",
    )(*sources)


def shift(value, axis, step):
    pairs = []
    for z in range(SIDE):
        for y in range(SIDE):
            to = (z * SIDE + (y + step) % SIDE) if axis == "y" else ((z + step) % SIDE) * SIDE + y
            pairs.append((z * SIDE + y, to))
    return lax.ppermute(value, "col", pairs)


def shift_x(value, step):
    pairs = [(2 * x + k, 2 * ((x + step) % SIDE) + k) for x in range(SIDE) for k in range(2)]
    return lax.ppermute(value, "row", pairs)


def swap_cores(value):
    return lax.ppermute(value, "row", [(i, i ^ 1) for i in range(2 * SIDE)])


def ring_place(away):
    return jnp.where(away == 0, 0, jnp.where(away == 3, 1, away + 1))


def plan_kernel(first_ref, second_ref, owner_ref, taper_ref, a_ref, b_ref, slot_ref, weight_ref):
    me, row = lax.axis_index("col"), lax.axis_index("row")
    station = first_ref[...]
    home, local = station >> 7, station & 127
    place_z = ring_place(((home >> 2) - (me >> 2)) & 3)
    place_y = ring_place(((home & 3) - (me & 3)) & 3)
    over_y = jnp.where(place_y == 0, place_z, 3 + 3 * place_z + place_y)
    over_z = jnp.where(place_z == 0, place_y, 3 + 3 * place_y + place_z)
    a_ref[...] = jnp.where(local < 64, over_y, 16 + over_z) * 64 + (local & 63)

    station = second_ref[...]
    home = station >> 7
    place_x = ring_place(((home >> 1) - (row >> 1)) & 3)
    b_ref[...] = (((home ^ row) & 1) * SIDE + place_x) * STA + (station & 127)

    owner = owner_ref[...]
    named = lax.broadcasted_iota(jnp.int32, (OWNERS, PAIRS), 0) == owner
    before = lax.broadcasted_iota(jnp.int32, (PAIRS, PAIRS), 0) < lax.broadcasted_iota(
        jnp.int32, (PAIRS, PAIRS), 1
    )
    counts = jnp.dot(
        jnp.where(named, 1.0, 0.0).astype(jnp.bfloat16),
        jnp.where(before, 1.0, 0.0).astype(jnp.bfloat16),
        preferred_element_type=jnp.float32,
    )
    rank = jnp.sum(jnp.where(named, counts, 0.0), axis=0, keepdims=True).astype(jnp.int32)
    slot_ref[...] = owner * (8 * CAP) + rank

    taper = taper_ref[...]
    lane = lax.broadcasted_iota(jnp.int32, (128, 128), 0)
    at = 2 * lax.broadcasted_iota(jnp.int32, (128, 128), 1)
    picked = []
    for odd in range(2):
        low, high = [
            jnp.dot(
                taper,
                jnp.where(lane + offset == at + odd, 1.0, 0.0).astype(jnp.float32),
                preferred_element_type=jnp.float32,
                precision=lax.Precision.HIGHEST,
            )
            for offset in (0, 128)
        ]
        picked += [low[0:1] + high[1:2], low[2:3] + high[3:4]]
    weight_ref[...] = jnp.concatenate(picked + picked, 0)


def plan(pair_first, pair_second, pair_owner, band_taper):
    line = jax.ShapeDtypeStruct((1, PAIRS), jnp.int32)
    return pl.pallas_call(
        plan_kernel,
        out_shape=[line, line, line, jax.ShapeDtypeStruct((8, 128), jnp.float32)],
        in_specs=[VMEM] * 4,
        out_specs=[VMEM] * 4,
        compiler_params=pltpu.CompilerParams(vmem_limit_bytes=12 * 1024 * 1024),
        cost_estimate=pl.CostEstimate(flops=2**25, bytes_accessed=2**15, transcendentals=0),
        name="plan",
    )(
        pair_first.reshape(1, PAIRS),
        pair_second.reshape(1, PAIRS),
        pair_owner.reshape(1, PAIRS),
        band_taper.reshape(4, 128),
    )


A_PARTS = [(0, 0, HALF), (1, 0, HALF), (2, 0, HALF)]
A_PARTS += [(8, 3 * QUARTER, QUARTER), (9, 3 * QUARTER, QUARTER)]
A_PARTS += [(7, 0, 3 * HALF), (5, 0, 3 * HALF), (6, 0, 3 * HALF)]
A_PARTS += [(8, 0, 3 * QUARTER), (9, 0, 3 * QUARTER)]
A_PARTS += [(0, HALF, HALF), (3, HALF, HALF), (4, HALF, HALF)]
A_PARTS += [(13, 3 * QUARTER, QUARTER), (14, 3 * QUARTER, QUARTER)]
A_PARTS += [(12, 0, 3 * HALF), (10, 0, 3 * HALF), (11, 0, 3 * HALF)]
A_PARTS += [(13, 0, 3 * QUARTER), (14, 0, 3 * QUARTER)]
B_PARTS = [(i, 0, BLOCK) for i in (0, 15, 16, 17, 18, 19, 20, 21)]


def cross_kernel(first_ref, second_ref, slot_ref, taper_ref, *refs):
    out_ref, a_ref, b_ref, cross_ref = refs[22:]
    for whole_ref, parts in ((a_ref, A_PARTS), (b_ref, B_PARTS)):
        at = 0
        for piece, start, rows in parts:
            stations = rows // 16
            block = refs[piece][start : start + rows].reshape(stations, 16, 128)
            whole_ref[at : at + stations] = block
            at += stations
    cross_ref[: out_ref.shape[0]] = jnp.zeros(out_ref.shape, jnp.float32)
    taper = taper_ref[...]
    low = lax.broadcasted_iota(jnp.int32, (8, 128), 0) < 4
    signed = jnp.where(low, taper, -taper)
    unroll = 64

    def value(p):
        a = a_ref[first_ref[0, p]].astype(jnp.float32)
        b = b_ref[second_ref[0, p]].astype(jnp.float32)
        a0, a1, b0, b1 = a[:8], a[8:], b[:8], b[8:]
        same = a0 * b0 + a1 * b1
        swapped = a0 * pltpu.roll(b0, 4, 0) + a1 * pltpu.roll(b1, 4, 0)
        keep = jnp.where(low, same, swapped)
        move = jnp.where(low, swapped, same)
        return keep * signed + pltpu.roll(move, 4, 0) * taper

    def step(i, carry):
        for u in range(unroll):
            p = i * unroll + u
            cross_ref[pl.ds(slot_ref[0, p], 8, stride=CAP), :] = value(p)
        return carry

    lax.fori_loop(0, PAIRS // unroll, step, 0)
    out_ref[...] = cross_ref[: out_ref.shape[0]].astype(jnp.bfloat16)


def cross_rows(first, second, slot, taper, a_pieces, b_pieces):
    rows = OWNERS * CAP * 8
    return pl.pallas_call(
        cross_kernel,
        out_shape=jax.ShapeDtypeStruct((rows, 128), jnp.bfloat16),
        in_specs=[SMEM] * 3 + [VMEM] * 23,
        out_specs=VMEM,
        scratch_shapes=[
            pltpu.VMEM((2048, 16, 128), jnp.bfloat16),
            pltpu.VMEM((1024, 16, 128), jnp.bfloat16),
            pltpu.VMEM((rows + 8 * CAP, 128), jnp.float32),
        ],
        compiler_params=pltpu.CompilerParams(vmem_limit_bytes=20 * 1024 * 1024),
        cost_estimate=pl.CostEstimate(
            flops=16 * 1024 * 1024, bytes_accessed=15 * 2**20, transcendentals=0
        ),
        name="cross",
    )(first, second, slot, taper, *a_pieces, *b_pieces)


def inverse_kernel(cross_ref, table_ref, out_hbm, even_ref, odd_ref, lags_ref, sems):
    for s in range(OWNERS):
        rows = pl.ds(s * CAP, CAP)
        for to, columns in ((even_ref, (0, 1, 4, 5)), (odd_ref, (2, 3, 6, 7))):
            for i, j in enumerate(columns):
                to[rows, i * 128 : (i + 1) * 128] = cross_ref[s, j * CAP : (j + 1) * CAP, :]
    width = 256
    copies = []
    for n in range(0, L // 2, width):
        e = jnp.dot(
            even_ref[...], table_ref[0, :, n : n + width], preferred_element_type=jnp.float32
        )
        o = jnp.dot(
            odd_ref[...], table_ref[1, :, n : n + width], preferred_element_type=jnp.float32
        )
        for at, lags in ((n, e + o), (L // 2 + n, e - o)):
            columns = pl.ds(at, width)
            lags_ref[:, columns] = lags.astype(jnp.bfloat16)
            copies.append(
                pltpu.make_async_copy(
                    lags_ref.at[:, columns], out_hbm.at[:, columns], sems.at[len(copies)]
                )
            )
            copies[-1].start()
    for copy in copies:
        copy.wait()


def inverse(arrived):
    return pl.pallas_call(
        inverse_kernel,
        out_shape=jax.ShapeDtypeStruct((OWNERS * CAP, L), jnp.bfloat16),
        in_specs=[VMEM] * 2,
        out_specs=pl.BlockSpec(memory_space=pl.ANY),
        scratch_shapes=[
            pltpu.VMEM((OWNERS * CAP, BINS), jnp.bfloat16),
            pltpu.VMEM((OWNERS * CAP, BINS), jnp.bfloat16),
            pltpu.VMEM((OWNERS * CAP, L), jnp.bfloat16),
            pltpu.SemaphoreType.DMA((8,)),
        ],
        compiler_params=pltpu.CompilerParams(vmem_limit_bytes=40 * 1024 * 1024),
        cost_estimate=pl.CostEstimate(
            flops=2 * 1536 * 1024 * 1024, bytes_accessed=11 * 2**20, transcendentals=0
        ),
        name="inverse",
    )(arrived, jnp.asarray(inverse_tables()))


def body(traces, band_taper, pair_first, pair_second, pair_owner):
    first, second, slot, taper = plan(pair_first, pair_second, pair_owner, band_taper)
    whole = whiten(traces)

    together = lax.optimization_barrier
    y_before, y_after = shift(whole, "y", 1), shift(whole, "y", -1)
    z_before, z_after = shift(whole, "z", 1), shift(whole, "z", -1)
    before_x = shift_x(whole, 1)

    (low_y,), (high_y,) = pack([y_before], [(0, 0, QUARTER)]), pack([y_after], [(0, QUARTER, QUARTER)])
    (low_z,) = pack([z_before], [(0, HALF, QUARTER)])
    (high_z,) = pack([z_after], [(0, HALF + QUARTER, QUARTER)])
    far_y = [shift(low_y, "y", 1), shift(high_y, "y", -1)]
    far_z = [shift(low_z, "z", 1), shift(high_z, "z", -1)]

    def three(before, after, far, start):
        blocks = [(0, start, HALF), (1, start, HALF), (2, 0, QUARTER), (3, 0, QUARTER)]
        return pack([before, after, *far], blocks)[0]

    over_y, over_z = three(y_before, y_after, far_y, 0), three(z_before, z_after, far_z, HALF)
    from_z_before, from_z_after = shift(over_y, "z", 1), shift(over_y, "z", -1)
    from_y_before, from_y_after = shift(over_z, "y", 1), shift(over_z, "y", -1)
    from_here, before_x, _ = together((whole, before_x, over_y))
    after_x = shift_x(from_here, -1)
    from_here, after_x = together((from_here, after_x))
    far_x = shift_x(from_here, 2)

    def lower(three, block, start):
        return pack([three, block], [(0, 0, 3 * QUARTER), (1, start, QUARTER)])[0]

    def upper(three, block, start):
        rows = [(0, 3 * QUARTER, 3 * QUARTER), (1, start + QUARTER, QUARTER)]
        return pack([three, block], rows)[0]

    onward = [lower(from_z_before, z_before, 0), upper(from_z_after, z_after, 0)]
    onward += [lower(from_y_before, y_before, HALF), upper(from_y_after, y_after, HALF)]
    late = [shift(onward[0], "z", 1), shift(onward[1], "z", -1)]
    late += [shift(onward[2], "y", 1), shift(onward[3], "y", -1)]
    own_core = [whole, before_x, after_x, far_x]
    ready = together((*own_core, *onward))[:4]
    there = [swap_cores(block) for block in ready]
    a_pieces = [whole, z_before, z_after, y_before, y_after]
    a_pieces += [from_z_before, from_z_after, over_y, *late[:2]]
    a_pieces += [from_y_before, from_y_after, over_z, *late[2:]]
    b_pieces = [before_x, after_x, far_x, *there]

    cross = cross_rows(first, second, slot, taper, a_pieces, b_pieces)
    outgoing = cross.reshape(OWNERS, 8 * CAP, 128)
    arrived = lax.all_to_all(outgoing, "col", split_axis=0, concat_axis=0, tiled=True)
    return inverse(arrived)


def solution(mesh):
    in_specs = (
        P(("row", "col"), None, None),
        P(),
        P(("row", "col")),
        P(("row", "col")),
        P(("row", "col"), None),
    )
    out_specs = P(("row", "col"), None)
    return jax.shard_map(body, mesh=mesh, in_specs=in_specs, out_specs=out_specs, check_vma=False)
```

```python
import functools
import math

import jax
import jax.numpy as jnp
import ml_dtypes
import numpy as np
from jax import lax
from jax.experimental import pallas as pl
from jax.experimental.pallas import tpu as pltpu
from jax.sharding import PartitionSpec as P

L = 2048
BINS = 512
LOW_BIN = 8
STA = 128
CAP = 96
SIDE = 4
OWNERS = 16
PAIRS = 1024
CHUNKS = 2
BLOCK = STA * 16
HALF = BLOCK // 2
QUARTER = BLOCK // 4

VMEM = pl.BlockSpec(memory_space=pltpu.VMEM)
SMEM = pl.BlockSpec(memory_space=pltpu.SMEM)

EVEN = np.arange(0, BINS, 2)
ODD = np.arange(1, BINS, 2)


def forward_tables():
    t = np.arange(L)[:, None]
    k = LOW_BIN + np.arange(BINS)[None, :]
    phase = (t * k % L) * (2.0 * math.pi / L)
    re = np.cos(phase) / math.sqrt(L)
    im = -np.sin(phase) / math.sqrt(L)
    half = L // 2
    tables = []
    for bins in (EVEN, ODD):
        columns = []
        for g in range(2):
            chosen = bins[g * 128 : (g + 1) * 128]
            columns += [re[:half, chosen], im[:half, chosen]]
        tables.append(np.concatenate(columns, 1).reshape(CHUNKS, half // CHUNKS, BINS))
    return np.stack(tables, 1).astype(np.float32).astype(ml_dtypes.bfloat16)


def inverse_tables():
    t = np.arange(L // 2)[None, :]
    k = LOW_BIN + np.arange(BINS)[:, None]
    phase = (t * k % L) * (2.0 * math.pi / L)
    re = np.cos(phase) / math.sqrt(BINS)
    im = -np.sin(phase) / math.sqrt(BINS)
    even = np.concatenate([re[EVEN], im[EVEN]], 0)
    odd = np.concatenate([re[ODD], im[ODD]], 0)
    return np.stack([even, odd]).astype(np.float32).astype(ml_dtypes.bfloat16)


def whiten_kernel(x_hbm, table_hbm, out_ref, x_ref, table_ref, wide_ref, rows_ref, sems):
    load_x = pltpu.make_async_copy(x_hbm, x_ref, sems.at[0])
    load_x.start()
    loads = []
    for k in range(CHUNKS):
        load = pltpu.make_async_copy(table_hbm.at[k], table_ref.at[k], sems.at[1 + k])
        load.start()
        loads.append(load)
    load_x.wait()
    wide_ref[...] = x_ref[...].astype(jnp.float32)
    spectra = [None, None]
    for k in range(CHUNKS):
        sums, differences = [], []
        for segment in range(2):
            added, taken = [], []
            for i in range(8 // CHUNKS * k, 8 // CHUNKS * (k + 1)):
                first = wide_ref[pl.ds(2 * i + segment, STA, stride=32), :]
                second = wide_ref[pl.ds(2 * (i + 8) + segment, STA, stride=32), :]
                added.append(first + second)
                taken.append(first - second)
            sums.append(jnp.concatenate(added, 1))
            differences.append(jnp.concatenate(taken, 1))
        loads[k].wait()
        for parity, rows in enumerate((sums, differences)):
            rows = jnp.concatenate(rows, 0)
            coarse = rows.astype(jnp.bfloat16)
            fine = (rows - coarse.astype(jnp.float32)).astype(jnp.bfloat16)
            part = jnp.dot(coarse, table_ref[k, parity], preferred_element_type=jnp.float32)
            part += jnp.dot(fine, table_ref[k, parity], preferred_element_type=jnp.float32)
            spectra[parity] = part if k == 0 else spectra[parity] + part
    lane_r = lax.broadcasted_iota(jnp.int32, (128, 128), 0)
    lane_c = lax.broadcasted_iota(jnp.int32, (128, 128), 1)
    group = jnp.where((lane_r >> 5) == (lane_c >> 5), 1.0 / 64.0, 0.0).astype(jnp.bfloat16)
    for g in range(2):
        parts = [
            spectra[parity][:, (2 * g + i) * 128 : (2 * g + i + 1) * 128]
            for i in range(2)
            for parity in range(2)
        ]
        power = sum(p * p for p in parts)
        coarse = power.astype(jnp.bfloat16)
        fine = (power - coarse.astype(jnp.float32)).astype(jnp.bfloat16)
        mean = jnp.dot(coarse, group, preferred_element_type=jnp.float32)
        mean += jnp.dot(fine, group, preferred_element_type=jnp.float32)
        scaling = lax.rsqrt(mean + 1e-06)
        for i, p in enumerate(parts):
            value = p * scaling
            for segment in range(2):
                rows_ref[pl.ds(8 * segment + 2 * i + g, STA, stride=16), :] = value[
                    segment * STA : (segment + 1) * STA
                ]
    out_ref[...] = rows_ref[...].astype(jnp.bfloat16)


def whiten(traces):
    rows = traces.reshape(STA, 2, L // 128, 128).transpose(0, 2, 1, 3).reshape(32 * STA, 128)
    return pl.pallas_call(
        whiten_kernel,
        out_shape=jax.ShapeDtypeStruct((BLOCK, 128), jnp.bfloat16),
        in_specs=[pl.BlockSpec(memory_space=pl.ANY)] * 2,
        out_specs=VMEM,
        scratch_shapes=[
            pltpu.VMEM((32 * STA, 128), jnp.bfloat16),
            pltpu.VMEM((CHUNKS, 2, L // 2 // CHUNKS, BINS), jnp.bfloat16),
            pltpu.VMEM((32 * STA, 128), jnp.float32),
            pltpu.VMEM((BLOCK, 128), jnp.float32),
            pltpu.SemaphoreType.DMA((1 + CHUNKS,)),
        ],
        compiler_params=pltpu.CompilerParams(vmem_limit_bytes=55 * 1024 * 1024),
        cost_estimate=pl.CostEstimate(
            flops=2 * 256 * L * 1024, bytes_accessed=6 * 2**20, transcendentals=0
        ),
        name="whiten",
    )(rows, jnp.asarray(forward_tables()))


def pack_kernel(plans, count, *refs):
    for plan, out in zip(plans, refs[count:]):
        at = 0
        for source, start, rows in plan:
            out[at : at + rows] = refs[source][start : start + rows]
            at += rows


def pack(sources, *plans):
    shapes = [
        jax.ShapeDtypeStruct((sum(rows for _, _, rows in plan), 128), jnp.bfloat16)
        for plan in plans
    ]
    size = 256 * sum(shape.shape[0] for shape in shapes)
    return pl.pallas_call(
        functools.partial(pack_kernel, plans, len(sources)),
        out_shape=shapes,
        in_specs=[VMEM] * len(sources),
        out_specs=[VMEM] * len(shapes),
        compiler_params=pltpu.CompilerParams(vmem_limit_bytes=2 * 1024 * 1024),
        cost_estimate=pl.CostEstimate(flops=0, bytes_accessed=2 * size, transcendentals=0),
        name="pack",
    )(*sources)


def shift(value, axis, step):
    pairs = []
    for z in range(SIDE):
        for y in range(SIDE):
            to = (z * SIDE + (y + step) % SIDE) if axis == "y" else ((z + step) % SIDE) * SIDE + y
            pairs.append((z * SIDE + y, to))
    return lax.ppermute(value, "col", pairs)


def shift_x(value, step):
    pairs = [(2 * x + k, 2 * ((x + step) % SIDE) + k) for x in range(SIDE) for k in range(2)]
    return lax.ppermute(value, "row", pairs)


def swap_cores(value):
    return lax.ppermute(value, "row", [(i, i ^ 1) for i in range(2 * SIDE)])


def ring_place(away):
    return jnp.where(away == 0, 0, jnp.where(away == 3, 1, away + 1))


def plan_kernel(first_ref, second_ref, owner_ref, taper_ref, a_ref, b_ref, slot_ref, weight_ref):
    me, row = lax.axis_index("col"), lax.axis_index("row")
    station = first_ref[...]
    home, local = station >> 7, station & 127
    place_z = ring_place(((home >> 2) - (me >> 2)) & 3)
    place_y = ring_place(((home & 3) - (me & 3)) & 3)
    over_y = jnp.where(place_y == 0, place_z, 3 + 3 * place_z + place_y)
    over_z = jnp.where(place_z == 0, place_y, 3 + 3 * place_y + place_z)
    a_ref[...] = jnp.where(local < 64, over_y, 16 + over_z) * 64 + (local & 63)

    station = second_ref[...]
    home = station >> 7
    place_x = ring_place(((home >> 1) - (row >> 1)) & 3)
    b_ref[...] = (((home ^ row) & 1) * SIDE + place_x) * STA + (station & 127)

    owner = owner_ref[...]
    named = lax.broadcasted_iota(jnp.int32, (OWNERS, PAIRS), 0) == owner
    before = lax.broadcasted_iota(jnp.int32, (PAIRS, PAIRS), 0) < lax.broadcasted_iota(
        jnp.int32, (PAIRS, PAIRS), 1
    )
    counts = jnp.dot(
        jnp.where(named, 1.0, 0.0).astype(jnp.bfloat16),
        jnp.where(before, 1.0, 0.0).astype(jnp.bfloat16),
        preferred_element_type=jnp.float32,
    )
    rank = jnp.sum(jnp.where(named, counts, 0.0), axis=0, keepdims=True).astype(jnp.int32)
    slot_ref[...] = owner * (8 * CAP) + rank

    taper = taper_ref[...]
    lane = lax.broadcasted_iota(jnp.int32, (128, 128), 0)
    at = 2 * lax.broadcasted_iota(jnp.int32, (128, 128), 1)
    picked = []
    for odd in range(2):
        low, high = [
            jnp.dot(
                taper,
                jnp.where(lane + offset == at + odd, 1.0, 0.0).astype(jnp.float32),
                preferred_element_type=jnp.float32,
                precision=lax.Precision.HIGHEST,
            )
            for offset in (0, 128)
        ]
        picked += [low[0:1] + high[1:2], low[2:3] + high[3:4]]
    weight_ref[...] = jnp.concatenate(picked + picked, 0)


def plan(pair_first, pair_second, pair_owner, band_taper):
    line = jax.ShapeDtypeStruct((1, PAIRS), jnp.int32)
    return pl.pallas_call(
        plan_kernel,
        out_shape=[line, line, line, jax.ShapeDtypeStruct((8, 128), jnp.float32)],
        in_specs=[VMEM] * 4,
        out_specs=[VMEM] * 4,
        compiler_params=pltpu.CompilerParams(vmem_limit_bytes=12 * 1024 * 1024),
        cost_estimate=pl.CostEstimate(flops=2**25, bytes_accessed=2**15, transcendentals=0),
        name="plan",
    )(
        pair_first.reshape(1, PAIRS),
        pair_second.reshape(1, PAIRS),
        pair_owner.reshape(1, PAIRS),
        band_taper.reshape(4, 128),
    )


A_PARTS = [(0, 0, HALF), (1, 0, HALF), (2, 0, HALF)]
A_PARTS += [(8, 3 * QUARTER, QUARTER), (9, 3 * QUARTER, QUARTER)]
A_PARTS += [(7, 0, 3 * HALF), (5, 0, 3 * HALF), (6, 0, 3 * HALF)]
A_PARTS += [(8, 0, 3 * QUARTER), (9, 0, 3 * QUARTER)]
A_PARTS += [(0, HALF, HALF), (3, HALF, HALF), (4, HALF, HALF)]
A_PARTS += [(13, 3 * QUARTER, QUARTER), (14, 3 * QUARTER, QUARTER)]
A_PARTS += [(12, 0, 3 * HALF), (10, 0, 3 * HALF), (11, 0, 3 * HALF)]
A_PARTS += [(13, 0, 3 * QUARTER), (14, 0, 3 * QUARTER)]
B_PARTS = [(i, 0, BLOCK) for i in (0, 15, 16, 17, 18, 19, 20, 21)]


def cross_kernel(first_ref, second_ref, slot_ref, taper_ref, *refs):
    out_ref, a_ref, b_ref, cross_ref = refs[22:]
    for whole_ref, parts in ((a_ref, A_PARTS), (b_ref, B_PARTS)):
        at = 0
        for piece, start, rows in parts:
            stations = rows // 16
            block = refs[piece][start : start + rows].reshape(stations, 16, 128)
            whole_ref[at : at + stations] = block
            at += stations
    cross_ref[: out_ref.shape[0]] = jnp.zeros(out_ref.shape, jnp.float32)
    taper = taper_ref[...]
    low = lax.broadcasted_iota(jnp.int32, (8, 128), 0) < 4
    signed = jnp.where(low, taper, -taper)
    unroll = 64

    def value(p):
        a = a_ref[first_ref[0, p]].astype(jnp.float32)
        b = b_ref[second_ref[0, p]].astype(jnp.float32)
        a0, a1, b0, b1 = a[:8], a[8:], b[:8], b[8:]
        same = a0 * b0 + a1 * b1
        swapped = a0 * pltpu.roll(b0, 4, 0) + a1 * pltpu.roll(b1, 4, 0)
        keep = jnp.where(low, same, swapped)
        move = jnp.where(low, swapped, same)
        return keep * signed + pltpu.roll(move, 4, 0) * taper

    def step(i, carry):
        for u in range(unroll):
            p = i * unroll + u
            cross_ref[pl.ds(slot_ref[0, p], 8, stride=CAP), :] = value(p)
        return carry

    lax.fori_loop(0, PAIRS // unroll, step, 0)
    out_ref[...] = cross_ref[: out_ref.shape[0]].astype(jnp.bfloat16)


def cross_rows(first, second, slot, taper, a_pieces, b_pieces):
    rows = OWNERS * CAP * 8
    return pl.pallas_call(
        cross_kernel,
        out_shape=jax.ShapeDtypeStruct((rows, 128), jnp.bfloat16),
        in_specs=[SMEM] * 3 + [VMEM] * 23,
        out_specs=VMEM,
        scratch_shapes=[
            pltpu.VMEM((2048, 16, 128), jnp.bfloat16),
            pltpu.VMEM((1024, 16, 128), jnp.bfloat16),
            pltpu.VMEM((rows + 8 * CAP, 128), jnp.float32),
        ],
        compiler_params=pltpu.CompilerParams(vmem_limit_bytes=20 * 1024 * 1024),
        cost_estimate=pl.CostEstimate(
            flops=16 * 1024 * 1024, bytes_accessed=15 * 2**20, transcendentals=0
        ),
        name="cross",
    )(first, second, slot, taper, *a_pieces, *b_pieces)


def inverse_kernel(cross_ref, table_ref, out_hbm, even_ref, odd_ref, lags_ref, sems):
    for s in range(OWNERS):
        rows = pl.ds(s * CAP, CAP)
        for to, columns in ((even_ref, (0, 1, 4, 5)), (odd_ref, (2, 3, 6, 7))):
            for i, j in enumerate(columns):
                to[rows, i * 128 : (i + 1) * 128] = cross_ref[s, j * CAP : (j + 1) * CAP, :]
    width = 256
    copies = []
    for n in range(0, L // 2, width):
        e = jnp.dot(
            even_ref[...], table_ref[0, :, n : n + width], preferred_element_type=jnp.float32
        )
        o = jnp.dot(
            odd_ref[...], table_ref[1, :, n : n + width], preferred_element_type=jnp.float32
        )
        for at, lags in ((n, e + o), (L // 2 + n, e - o)):
            columns = pl.ds(at, width)
            lags_ref[:, columns] = lags.astype(jnp.bfloat16)
            copies.append(
                pltpu.make_async_copy(
                    lags_ref.at[:, columns], out_hbm.at[:, columns], sems.at[len(copies)]
                )
            )
            copies[-1].start()
    for copy in copies:
        copy.wait()


def inverse(arrived):
    return pl.pallas_call(
        inverse_kernel,
        out_shape=jax.ShapeDtypeStruct((OWNERS * CAP, L), jnp.bfloat16),
        in_specs=[VMEM] * 2,
        out_specs=pl.BlockSpec(memory_space=pl.ANY),
        scratch_shapes=[
            pltpu.VMEM((OWNERS * CAP, BINS), jnp.bfloat16),
            pltpu.VMEM((OWNERS * CAP, BINS), jnp.bfloat16),
            pltpu.VMEM((OWNERS * CAP, L), jnp.bfloat16),
            pltpu.SemaphoreType.DMA((8,)),
        ],
        compiler_params=pltpu.CompilerParams(vmem_limit_bytes=40 * 1024 * 1024),
        cost_estimate=pl.CostEstimate(
            flops=2 * 1536 * 1024 * 1024, bytes_accessed=11 * 2**20, transcendentals=0
        ),
        name="inverse",
    )(arrived, jnp.asarray(inverse_tables()))


def body(traces, band_taper, pair_first, pair_second, pair_owner):
    first, second, slot, taper = plan(pair_first, pair_second, pair_owner, band_taper)
    whole = whiten(traces)

    together = lax.optimization_barrier
    y_before, y_after = shift(whole, "y", 1), shift(whole, "y", -1)
    z_before, z_after = shift(whole, "z", 1), shift(whole, "z", -1)
    before_x = shift_x(whole, 1)

    (low_y,), (high_y,) = pack([y_before], [(0, 0, QUARTER)]), pack([y_after], [(0, QUARTER, QUARTER)])
    (low_z,) = pack([z_before], [(0, HALF, QUARTER)])
    (high_z,) = pack([z_after], [(0, HALF + QUARTER, QUARTER)])
    far_y = [shift(low_y, "y", 1), shift(high_y, "y", -1)]
    far_z = [shift(low_z, "z", 1), shift(high_z, "z", -1)]

    def three(before, after, far, start):
        blocks = [(0, start, HALF), (1, start, HALF), (2, 0, QUARTER), (3, 0, QUARTER)]
        return pack([before, after, *far], blocks)[0]

    over_y, over_z = three(y_before, y_after, far_y, 0), three(z_before, z_after, far_z, HALF)
    from_z_before, from_z_after = shift(over_y, "z", 1), shift(over_y, "z", -1)
    from_y_before, from_y_after = shift(over_z, "y", 1), shift(over_z, "y", -1)
    from_here, before_x, _ = together((whole, before_x, over_y))
    after_x = shift_x(from_here, -1)
    from_here, after_x = together((from_here, after_x))
    far_x = shift_x(from_here, 2)

    def lower(three, block, start):
        return pack([three, block], [(0, 0, 3 * QUARTER), (1, start, QUARTER)])[0]

    def upper(three, block, start):
        rows = [(0, 3 * QUARTER, 3 * QUARTER), (1, start + QUARTER, QUARTER)]
        return pack([three, block], rows)[0]

    onward = [lower(from_z_before, z_before, 0), upper(from_z_after, z_after, 0)]
    onward += [lower(from_y_before, y_before, HALF), upper(from_y_after, y_after, HALF)]
    late = [shift(onward[0], "z", 1), shift(onward[1], "z", -1)]
    late += [shift(onward[2], "y", 1), shift(onward[3], "y", -1)]
    own_core = [whole, before_x, after_x, far_x]
    ready = together((*own_core, *onward))[:4]
    there = [swap_cores(block) for block in ready]
    a_pieces = [whole, z_before, z_after, y_before, y_after]
    a_pieces += [from_z_before, from_z_after, over_y, *late[:2]]
    a_pieces += [from_y_before, from_y_after, over_z, *late[2:]]
    b_pieces = [before_x, after_x, far_x, *there]

    cross = cross_rows(first, second, slot, taper, a_pieces, b_pieces)
    outgoing = cross.reshape(OWNERS, 8 * CAP, 128)
    arrived = lax.all_to_all(outgoing, "col", split_axis=0, concat_axis=0, tiled=True)
    return inverse(arrived)


def solution(mesh):
    in_specs = (
        P(("row", "col"), None, None),
        P(),
        P(("row", "col")),
        P(("row", "col")),
        P(("row", "col"), None),
    )
    out_specs = P(("row", "col"), None)
    return jax.shard_map(body, mesh=mesh, in_specs=in_specs, out_specs=out_specs, check_vma=False)
```

```python
import functools
import math

import jax
import jax.numpy as jnp
import ml_dtypes
import numpy as np
from jax import lax
from jax.experimental import pallas as pl
from jax.experimental.pallas import tpu as pltpu
from jax.sharding import PartitionSpec as P

L = 2048
BINS = 512
LOW_BIN = 8
STA = 128
CAP = 96
SIDE = 4
OWNERS = 16
PAIRS = 1024
CHUNKS = 2
BLOCK = STA * 16
HALF = BLOCK // 2
QUARTER = BLOCK // 4

VMEM = pl.BlockSpec(memory_space=pltpu.VMEM)
SMEM = pl.BlockSpec(memory_space=pltpu.SMEM)

EVEN = np.arange(0, BINS, 2)
ODD = np.arange(1, BINS, 2)


def forward_tables():
    t = np.arange(L)[:, None]
    k = LOW_BIN + np.arange(BINS)[None, :]
    phase = (t * k % L) * (2.0 * math.pi / L)
    re = np.cos(phase) / math.sqrt(L)
    im = -np.sin(phase) / math.sqrt(L)
    half = L // 2
    tables = []
    for bins in (EVEN, ODD):
        columns = []
        for g in range(2):
            chosen = bins[g * 128 : (g + 1) * 128]
            columns += [re[:half, chosen], im[:half, chosen]]
        tables.append(np.concatenate(columns, 1).reshape(CHUNKS, half // CHUNKS, BINS))
    return np.stack(tables, 1).astype(np.float32).astype(ml_dtypes.bfloat16)


def inverse_tables():
    t = np.arange(L // 2)[None, :]
    k = LOW_BIN + np.arange(BINS)[:, None]
    phase = (t * k % L) * (2.0 * math.pi / L)
    re = np.cos(phase) / math.sqrt(BINS)
    im = -np.sin(phase) / math.sqrt(BINS)
    even = np.concatenate([re[EVEN], im[EVEN]], 0)
    odd = np.concatenate([re[ODD], im[ODD]], 0)
    return np.stack([even, odd]).astype(np.float32).astype(ml_dtypes.bfloat16)


def whiten_kernel(x_hbm, table_hbm, out_ref, x_ref, table_ref, wide_ref, rows_ref, sems):
    load_x = pltpu.make_async_copy(x_hbm, x_ref, sems.at[0])
    load_x.start()
    loads = []
    for k in range(CHUNKS):
        load = pltpu.make_async_copy(table_hbm.at[k], table_ref.at[k], sems.at[1 + k])
        load.start()
        loads.append(load)
    load_x.wait()
    wide_ref[...] = x_ref[...].astype(jnp.float32)
    spectra = [None, None]
    for k in range(CHUNKS):
        sums, differences = [], []
        for segment in range(2):
            added, taken = [], []
            for i in range(8 // CHUNKS * k, 8 // CHUNKS * (k + 1)):
                first = wide_ref[pl.ds(2 * i + segment, STA, stride=32), :]
                second = wide_ref[pl.ds(2 * (i + 8) + segment, STA, stride=32), :]
                added.append(first + second)
                taken.append(first - second)
            sums.append(jnp.concatenate(added, 1))
            differences.append(jnp.concatenate(taken, 1))
        loads[k].wait()
        for parity, rows in enumerate((sums, differences)):
            rows = jnp.concatenate(rows, 0)
            coarse = rows.astype(jnp.bfloat16)
            fine = (rows - coarse.astype(jnp.float32)).astype(jnp.bfloat16)
            terms = jnp.concatenate([coarse, fine], 0)
            part = jnp.dot(terms, table_ref[k, parity], preferred_element_type=jnp.float32)
            part = part[: 2 * STA] + part[2 * STA :]
            spectra[parity] = part if k == 0 else spectra[parity] + part
    lane_r = lax.broadcasted_iota(jnp.int32, (128, 128), 0)
    lane_c = lax.broadcasted_iota(jnp.int32, (128, 128), 1)
    group = jnp.where((lane_r >> 5) == (lane_c >> 5), 1.0 / 64.0, 0.0).astype(jnp.bfloat16)
    for g in range(2):
        parts = [
            spectra[parity][:, (2 * g + i) * 128 : (2 * g + i + 1) * 128]
            for i in range(2)
            for parity in range(2)
        ]
        power = sum(p * p for p in parts)
        coarse = power.astype(jnp.bfloat16)
        fine = (power - coarse.astype(jnp.float32)).astype(jnp.bfloat16)
        mean = jnp.dot(coarse, group, preferred_element_type=jnp.float32)
        mean += jnp.dot(fine, group, preferred_element_type=jnp.float32)
        scaling = lax.rsqrt(mean + 1e-06)
        for i, p in enumerate(parts):
            value = p * scaling
            for segment in range(2):
                rows_ref[pl.ds(8 * segment + 2 * i + g, STA, stride=16), :] = value[
                    segment * STA : (segment + 1) * STA
                ]
    out_ref[...] = rows_ref[...].astype(jnp.bfloat16)


def whiten(traces):
    rows = traces.reshape(STA, 2, L // 128, 128).transpose(0, 2, 1, 3).reshape(32 * STA, 128)
    return pl.pallas_call(
        whiten_kernel,
        out_shape=jax.ShapeDtypeStruct((BLOCK, 128), jnp.bfloat16),
        in_specs=[pl.BlockSpec(memory_space=pl.ANY)] * 2,
        out_specs=VMEM,
        scratch_shapes=[
            pltpu.VMEM((32 * STA, 128), jnp.bfloat16),
            pltpu.VMEM((CHUNKS, 2, L // 2 // CHUNKS, BINS), jnp.bfloat16),
            pltpu.VMEM((32 * STA, 128), jnp.float32),
            pltpu.VMEM((BLOCK, 128), jnp.float32),
            pltpu.SemaphoreType.DMA((1 + CHUNKS,)),
        ],
        compiler_params=pltpu.CompilerParams(vmem_limit_bytes=55 * 1024 * 1024),
        cost_estimate=pl.CostEstimate(
            flops=2 * 256 * L * 1024, bytes_accessed=6 * 2**20, transcendentals=0
        ),
        name="whiten",
    )(rows, jnp.asarray(forward_tables()))


def pack_kernel(plans, count, *refs):
    for plan, out in zip(plans, refs[count:]):
        at = 0
        for source, start, rows in plan:
            out[at : at + rows] = refs[source][start : start + rows]
            at += rows


def pack(sources, *plans):
    shapes = [
        jax.ShapeDtypeStruct((sum(rows for _, _, rows in plan), 128), jnp.bfloat16)
        for plan in plans
    ]
    size = 256 * sum(shape.shape[0] for shape in shapes)
    return pl.pallas_call(
        functools.partial(pack_kernel, plans, len(sources)),
        out_shape=shapes,
        in_specs=[VMEM] * len(sources),
        out_specs=[VMEM] * len(shapes),
        compiler_params=pltpu.CompilerParams(vmem_limit_bytes=2 * 1024 * 1024),
        cost_estimate=pl.CostEstimate(flops=0, bytes_accessed=2 * size, transcendentals=0),
        name="pack",
    )(*sources)


def shift(value, axis, step):
    pairs = []
    for z in range(SIDE):
        for y in range(SIDE):
            to = (z * SIDE + (y + step) % SIDE) if axis == "y" else ((z + step) % SIDE) * SIDE + y
            pairs.append((z * SIDE + y, to))
    return lax.ppermute(value, "col", pairs)


def shift_x(value, step):
    pairs = [(2 * x + k, 2 * ((x + step) % SIDE) + k) for x in range(SIDE) for k in range(2)]
    return lax.ppermute(value, "row", pairs)


def swap_cores(value):
    return lax.ppermute(value, "row", [(i, i ^ 1) for i in range(2 * SIDE)])


def ring_place(away):
    return jnp.where(away == 0, 0, jnp.where(away == 3, 1, away + 1))


def plan_kernel(first_ref, second_ref, owner_ref, taper_ref, a_ref, b_ref, slot_ref, weight_ref):
    me, row = lax.axis_index("col"), lax.axis_index("row")
    station = first_ref[...]
    home, local = station >> 7, station & 127
    place_z = ring_place(((home >> 2) - (me >> 2)) & 3)
    place_y = ring_place(((home & 3) - (me & 3)) & 3)
    over_y = jnp.where(place_y == 0, place_z, 3 + 3 * place_z + place_y)
    over_z = jnp.where(place_z == 0, place_y, 3 + 3 * place_y + place_z)
    a_ref[...] = jnp.where(local < 64, over_y, 16 + over_z) * 64 + (local & 63)

    station = second_ref[...]
    home = station >> 7
    place_x = ring_place(((home >> 1) - (row >> 1)) & 3)
    b_ref[...] = (((home ^ row) & 1) * SIDE + place_x) * STA + (station & 127)

    owner = owner_ref[...]
    named = lax.broadcasted_iota(jnp.int32, (OWNERS, PAIRS), 0) == owner
    before = lax.broadcasted_iota(jnp.int32, (PAIRS, PAIRS), 0) < lax.broadcasted_iota(
        jnp.int32, (PAIRS, PAIRS), 1
    )
    counts = jnp.dot(
        jnp.where(named, 1.0, 0.0).astype(jnp.bfloat16),
        jnp.where(before, 1.0, 0.0).astype(jnp.bfloat16),
        preferred_element_type=jnp.float32,
    )
    rank = jnp.sum(jnp.where(named, counts, 0.0), axis=0, keepdims=True).astype(jnp.int32)
    slot_ref[...] = owner * (8 * CAP) + rank

    taper = taper_ref[...]
    lane = lax.broadcasted_iota(jnp.int32, (128, 128), 0)
    at = 2 * lax.broadcasted_iota(jnp.int32, (128, 128), 1)
    picked = []
    for odd in range(2):
        low, high = [
            jnp.dot(
                taper,
                jnp.where(lane + offset == at + odd, 1.0, 0.0).astype(jnp.float32),
                preferred_element_type=jnp.float32,
                precision=lax.Precision.HIGHEST,
            )
            for offset in (0, 128)
        ]
        picked += [low[0:1] + high[1:2], low[2:3] + high[3:4]]
    weight_ref[...] = jnp.concatenate(picked + picked, 0)


def plan(pair_first, pair_second, pair_owner, band_taper):
    line = jax.ShapeDtypeStruct((1, PAIRS), jnp.int32)
    return pl.pallas_call(
        plan_kernel,
        out_shape=[line, line, line, jax.ShapeDtypeStruct((8, 128), jnp.float32)],
        in_specs=[VMEM] * 4,
        out_specs=[VMEM] * 4,
        compiler_params=pltpu.CompilerParams(vmem_limit_bytes=12 * 1024 * 1024),
        cost_estimate=pl.CostEstimate(flops=2**25, bytes_accessed=2**15, transcendentals=0),
        name="plan",
    )(
        pair_first.reshape(1, PAIRS),
        pair_second.reshape(1, PAIRS),
        pair_owner.reshape(1, PAIRS),
        band_taper.reshape(4, 128),
    )


A_PARTS = [(0, 0, HALF), (1, 0, HALF), (2, 0, HALF)]
A_PARTS += [(8, 3 * QUARTER, QUARTER), (9, 3 * QUARTER, QUARTER)]
A_PARTS += [(7, 0, 3 * HALF), (5, 0, 3 * HALF), (6, 0, 3 * HALF)]
A_PARTS += [(8, 0, 3 * QUARTER), (9, 0, 3 * QUARTER)]
A_PARTS += [(0, HALF, HALF), (3, HALF, HALF), (4, HALF, HALF)]
A_PARTS += [(13, 3 * QUARTER, QUARTER), (14, 3 * QUARTER, QUARTER)]
A_PARTS += [(12, 0, 3 * HALF), (10, 0, 3 * HALF), (11, 0, 3 * HALF)]
A_PARTS += [(13, 0, 3 * QUARTER), (14, 0, 3 * QUARTER)]
B_PARTS = [(i, 0, BLOCK) for i in (0, 15, 16, 17, 18, 19, 20, 21)]


def cross_kernel(first_ref, second_ref, slot_ref, taper_ref, *refs):
    out_ref, a_ref, b_ref, cross_ref = refs[22:]
    for whole_ref, parts in ((a_ref, A_PARTS), (b_ref, B_PARTS)):
        at = 0
        for piece, start, rows in parts:
            stations = rows // 16
            block = refs[piece][start : start + rows].reshape(stations, 16, 128)
            whole_ref[at : at + stations] = block
            at += stations
    cross_ref[: out_ref.shape[0]] = jnp.zeros(out_ref.shape, jnp.float32)
    taper = taper_ref[...]
    low = lax.broadcasted_iota(jnp.int32, (8, 128), 0) < 4
    signed = jnp.where(low, taper, -taper)
    unroll = 64

    def value(p):
        a = a_ref[first_ref[0, p]].astype(jnp.float32)
        b = b_ref[second_ref[0, p]].astype(jnp.float32)
        a0, a1, b0, b1 = a[:8], a[8:], b[:8], b[8:]
        same = a0 * b0 + a1 * b1
        swapped = a0 * pltpu.roll(b0, 4, 0) + a1 * pltpu.roll(b1, 4, 0)
        keep = jnp.where(low, same, swapped)
        move = jnp.where(low, swapped, same)
        return keep * signed + pltpu.roll(move, 4, 0) * taper

    def step(i, carry):
        for u in range(unroll):
            p = i * unroll + u
            cross_ref[pl.ds(slot_ref[0, p], 8, stride=CAP), :] = value(p)
        return carry

    lax.fori_loop(0, PAIRS // unroll, step, 0)
    out_ref[...] = cross_ref[: out_ref.shape[0]].astype(jnp.bfloat16)


def cross_rows(first, second, slot, taper, a_pieces, b_pieces):
    rows = OWNERS * CAP * 8
    return pl.pallas_call(
        cross_kernel,
        out_shape=jax.ShapeDtypeStruct((rows, 128), jnp.bfloat16),
        in_specs=[SMEM] * 3 + [VMEM] * 23,
        out_specs=VMEM,
        scratch_shapes=[
            pltpu.VMEM((2048, 16, 128), jnp.bfloat16),
            pltpu.VMEM((1024, 16, 128), jnp.bfloat16),
            pltpu.VMEM((rows + 8 * CAP, 128), jnp.float32),
        ],
        compiler_params=pltpu.CompilerParams(vmem_limit_bytes=20 * 1024 * 1024),
        cost_estimate=pl.CostEstimate(
            flops=16 * 1024 * 1024, bytes_accessed=15 * 2**20, transcendentals=0
        ),
        name="cross",
    )(first, second, slot, taper, *a_pieces, *b_pieces)


def inverse_kernel(cross_ref, table_ref, out_hbm, even_ref, odd_ref, lags_ref, sems):
    for s in range(OWNERS):
        rows = pl.ds(s * CAP, CAP)
        for to, columns in ((even_ref, (0, 1, 4, 5)), (odd_ref, (2, 3, 6, 7))):
            for i, j in enumerate(columns):
                to[rows, i * 128 : (i + 1) * 128] = cross_ref[s, j * CAP : (j + 1) * CAP, :]
    width = 256
    copies = []
    for n in range(0, L // 2, width):
        e = jnp.dot(
            even_ref[...], table_ref[0, :, n : n + width], preferred_element_type=jnp.float32
        )
        o = jnp.dot(
            odd_ref[...], table_ref[1, :, n : n + width], preferred_element_type=jnp.float32
        )
        for at, lags in ((n, e + o), (L // 2 + n, e - o)):
            columns = pl.ds(at, width)
            lags_ref[:, columns] = lags.astype(jnp.bfloat16)
            copies.append(
                pltpu.make_async_copy(
                    lags_ref.at[:, columns], out_hbm.at[:, columns], sems.at[len(copies)]
                )
            )
            copies[-1].start()
    for copy in copies:
        copy.wait()


def inverse(arrived):
    return pl.pallas_call(
        inverse_kernel,
        out_shape=jax.ShapeDtypeStruct((OWNERS * CAP, L), jnp.bfloat16),
        in_specs=[VMEM] * 2,
        out_specs=pl.BlockSpec(memory_space=pl.ANY),
        scratch_shapes=[
            pltpu.VMEM((OWNERS * CAP, BINS), jnp.bfloat16),
            pltpu.VMEM((OWNERS * CAP, BINS), jnp.bfloat16),
            pltpu.VMEM((OWNERS * CAP, L), jnp.bfloat16),
            pltpu.SemaphoreType.DMA((8,)),
        ],
        compiler_params=pltpu.CompilerParams(vmem_limit_bytes=40 * 1024 * 1024),
        cost_estimate=pl.CostEstimate(
            flops=2 * 1536 * 1024 * 1024, bytes_accessed=11 * 2**20, transcendentals=0
        ),
        name="inverse",
    )(arrived, jnp.asarray(inverse_tables()))


def body(traces, band_taper, pair_first, pair_second, pair_owner):
    first, second, slot, taper = plan(pair_first, pair_second, pair_owner, band_taper)
    whole = whiten(traces)

    together = lax.optimization_barrier
    y_before, y_after = shift(whole, "y", 1), shift(whole, "y", -1)
    z_before, z_after = shift(whole, "z", 1), shift(whole, "z", -1)
    before_x = shift_x(whole, 1)

    (low_y,), (high_y,) = pack([y_before], [(0, 0, QUARTER)]), pack([y_after], [(0, QUARTER, QUARTER)])
    (low_z,) = pack([z_before], [(0, HALF, QUARTER)])
    (high_z,) = pack([z_after], [(0, HALF + QUARTER, QUARTER)])
    far_y = [shift(low_y, "y", 1), shift(high_y, "y", -1)]
    far_z = [shift(low_z, "z", 1), shift(high_z, "z", -1)]

    def three(before, after, far, start):
        blocks = [(0, start, HALF), (1, start, HALF), (2, 0, QUARTER), (3, 0, QUARTER)]
        return pack([before, after, *far], blocks)[0]

    over_y, over_z = three(y_before, y_after, far_y, 0), three(z_before, z_after, far_z, HALF)
    from_z_before, from_z_after = shift(over_y, "z", 1), shift(over_y, "z", -1)
    from_y_before, from_y_after = shift(over_z, "y", 1), shift(over_z, "y", -1)
    from_here, before_x, _ = together((whole, before_x, over_y))
    after_x = shift_x(from_here, -1)
    from_here, after_x = together((from_here, after_x))
    far_x = shift_x(from_here, 2)

    def lower(three, block, start):
        return pack([three, block], [(0, 0, 3 * QUARTER), (1, start, QUARTER)])[0]

    def upper(three, block, start):
        rows = [(0, 3 * QUARTER, 3 * QUARTER), (1, start + QUARTER, QUARTER)]
        return pack([three, block], rows)[0]

    onward = [lower(from_z_before, z_before, 0), upper(from_z_after, z_after, 0)]
    onward += [lower(from_y_before, y_before, HALF), upper(from_y_after, y_after, HALF)]
    late = [shift(onward[0], "z", 1), shift(onward[1], "z", -1)]
    late += [shift(onward[2], "y", 1), shift(onward[3], "y", -1)]
    own_core = [whole, before_x, after_x, far_x]
    ready = together((*own_core, *onward))[:4]
    there = [swap_cores(block) for block in ready]
    a_pieces = [whole, z_before, z_after, y_before, y_after]
    a_pieces += [from_z_before, from_z_after, over_y, *late[:2]]
    a_pieces += [from_y_before, from_y_after, over_z, *late[2:]]
    b_pieces = [before_x, after_x, far_x, *there]

    cross = cross_rows(first, second, slot, taper, a_pieces, b_pieces)
    outgoing = cross.reshape(OWNERS, 8 * CAP, 128)
    arrived = lax.all_to_all(outgoing, "col", split_axis=0, concat_axis=0, tiled=True)
    return inverse(arrived)


def solution(mesh):
    in_specs = (
        P(("row", "col"), None, None),
        P(),
        P(("row", "col")),
        P(("row", "col")),
        P(("row", "col"), None),
    )
    out_specs = P(("row", "col"), None)
    return jax.shard_map(body, mesh=mesh, in_specs=in_specs, out_specs=out_specs, check_vma=False)
```
